32 devices in a mesh: ep: 8 (over z, x), etp: 4 (over y, core).
Axes of the slice: x: 2, y: 2, z: 4, core: 2. Of those that a mesh axis runs over, the one named last changes fastest.
Arguments:
- tokens: bfloat16 [1024, 3072], P('ep', 'etp'), may hold values from -6 to 6
- grad_out: bfloat16 [1024, 3072], P('ep', 'etp'), may hold values from -6 to 6
- probs: float32 [1024, 4], P('ep'), may hold values from 0.1 to 1
- expert_ids: int32 [1024, 4], P('ep'), may hold values from 0 to 7, all different within a row; in each aligned block of 128 rows (0 to 127, 128 to 255, ...) at most 96 rows name the same one
- w_gate: bfloat16 [8, 3072, 5376], P('ep', None, 'etp'), may hold values from -0.109375 to 0.109375
- w_up: bfloat16 [8, 3072, 5376], P('ep', None, 'etp'), may hold values from -0.109375 to 0.109375
- w_down: bfloat16 [8, 5376, 3072], P('ep', 'etp'), may hold values from -0.078125 to 0.078125
Outputs:
- grad_tokens: bfloat16 [1024, 3072], P('ep', 'etp')
- grad_gate: bfloat16 [8, 3072, 5376], P('ep', None, 'etp')
- grad_up: bfloat16 [8, 3072, 5376], P('ep', None, 'etp')
- grad_down: bfloat16 [8, 5376, 3072], P('ep', 'etp')
The draws below stay inside these ranges and needn't reach their ends.
Inputs may be any that keep to these rules, and one draw needn't show every extreme that they name: `expert_ids`: each row names 4 different experts. In the rows of one index of ep (aligned blocks of 128 rows) no expert is named by more than 96 rows, a bound that some block reaches.
All inputs are finite; a program needn't handle non-finite values.
Results may differ from the reference program's by a relative error of at most 0.02.
Values may be sent and summed in bfloat16 or wider, within the bound.
No kernel may reach another device: no remote copies, remote signals or barrier semaphores. Data moves between devices by JAX's collectives and lax.ppermute only.
A program may use at most 128 MiB of HBM per device.

```python
import math
import jax
import jax.numpy as jnp
import numpy as np
from jax import lax

D = 3072
FF = 5376
TOPK = 4
TOK_DEV = 128
EXPERTS = 8
CAP = 96
ROWS = 768
FF_DEV = 1344
TOKENS = 1024


def block_scale(key, shape, pieces, low, largest):
    gain = 1.0
    for axis_at, parts in pieces:
        heights = jax.random.uniform(jax.random.fold_in(jax.random.fold_in(key, 6), axis_at), (parts,), jnp.float32, low / len(pieces), largest / len(pieces))
        gain = gain * jnp.repeat(jnp.exp(heights), shape[axis_at] // parts).reshape((-1,) + (1,) * (len(shape) - 1 - axis_at))
    return gain


def shared_out(own_key, own, number, rows, count, top, reach, lean):
    order = jax.random.permutation(own_key, count)
    crowded, common = portions_of(count, rows * top, reach, lean, True), portions_of(count, rows * top, reach, lean, False)
    places = jnp.arange(count)

    def named(lengths, offset_by):
        used = int((lengths > 0).sum())
        fixed = max(1, used // 4)
        shifted = fixed + (places - fixed + offset_by * (used - fixed)) % max(1, count - fixed)
        return jnp.zeros((count,), jnp.int32).at[order[jnp.where(places < fixed, places, shifted)]].set(jnp.asarray(lengths, jnp.int32))

    lengths = jnp.where(number % 4 == 0, named(crowded, number // 4), named(common, number - number // 4 - 1))
    mixed = jax.random.permutation(jax.random.fold_in(own, 3), count)
    donor, sink = mixed[0:count // 2 * 2:2], mixed[1:count // 2 * 2:2]
    margin = jnp.minimum(lengths[donor] - 1, reach - lengths[sink]) // 2
    margin = jnp.where((donor == order[0]) | (sink == order[0]) | (lengths[sink] == 0), 0, jnp.maximum(margin, 0))
    shifted = jax.random.randint(jax.random.fold_in(own, 4), (count // 2,), 0, 1 << 20) % (margin + 1)
    lengths = lengths.at[donor].add(-shifted).at[sink].add(shifted)
    members = jnp.searchsorted(jnp.cumsum(lengths), jnp.arange(rows * top), side="right").astype(jnp.int32)
    table = members.reshape(top, rows).T
    table = table[jax.random.permutation(jax.random.fold_in(own, 1), rows)]
    offset_by = jax.random.randint(jax.random.fold_in(own, 2), (rows, 1), 0, top)
    return jnp.take_along_axis(table, (jnp.arange(top)[None, :] + offset_by) % top, axis=1)


def portions_of(amount, total, reach, lean, full):
    portions = [(1 << 20) // math.isqrt(rank ** lean) + 1 for rank in range(1, amount + 1)]
    largest = reach if full else min(reach, max(-(-total // amount), total * portions[0] // sum(portions)))
    least = 1 if total - largest >= amount - 1 else 0
    holding, spare = [largest] + [least] * (amount - 1), total - largest - least * (amount - 1)
    while spare > 0:
        free = [i for i in range(1, amount) if holding[i] < largest] or [i for i in range(1, amount) if holding[i] < reach]
        whole, left = sum([portions[i] for i in free]), spare
        for i in free:
            extra = min(reach - holding[i], max(1, left * portions[i] // whole), spare)
            holding[i] = holding[i] + extra
            spare = spare - extra
    return np.array(holding)


def scatter_about(stream_key, extent, spread, bound, pieces=(), held_as=jnp.bfloat16):
    array = spread * jax.random.normal(stream_key, extent, jnp.float32)
    if pieces:
        array = array * block_scale(stream_key, extent, pieces, -0.22, 0.18)
    return jnp.clip(array, -bound, bound).astype(held_as)


def setup_inputs(seed: int = 0) -> dict:
    key_list = jax.random.split(jax.random.key(seed), 8)
    tokens = scatter_about(key_list[0], (TOKENS, D), 1.0, 6.0, ((0, 8), (1, 4)))
    grad_out = scatter_about(key_list[1], (TOKENS, D), 1.0, 6.0, ((0, 8), (1, 4)))
    probs = jnp.clip(0.1 + 0.9 * jax.random.uniform(key_list[2], (TOKENS, TOPK), jnp.float32) ** block_scale(key_list[2], (TOKENS, TOPK), ((0, 8),), -0.2, 0.2), 0.1, 1.0)
    expert_ids_keys = jax.random.split(jax.random.fold_in(key_list[3], 1), TOKENS // TOK_DEV)
    expert_ids_turns = jax.random.permutation(jax.random.fold_in(key_list[3], 3), TOKENS // TOK_DEV)
    expert_ids = jax.vmap(lambda own, number: shared_out(jax.random.fold_in(key_list[3], 2), own, number, TOK_DEV, EXPERTS, TOPK, CAP, 2))(expert_ids_keys, expert_ids_turns).reshape((TOKENS, TOPK))
    w_gate = scatter_about(key_list[4], (EXPERTS, D, FF), D ** -0.5, 0.109375, ((0, 8), (2, 4)))
    w_up = scatter_about(key_list[5], (EXPERTS, D, FF), D ** -0.5, 0.109375, ((0, 8), (2, 4)))
    w_down = scatter_about(key_list[6], (EXPERTS, FF, D), FF ** -0.5, 0.078125, ((0, 8), (1, 4)))
    return {"tokens": tokens, "grad_out": grad_out, "probs": probs, "expert_ids": expert_ids, "w_gate": w_gate, "w_up": w_up, "w_down": w_down}


def slot_index(block_ids, capacity, expert_count):
    flat_ids = block_ids.reshape(-1).astype(jnp.int32)
    onehot = (flat_ids[:, None] == jnp.arange(expert_count, dtype=jnp.int32)[None, :]).astype(jnp.int32)
    earlier = jnp.cumsum(onehot, axis=0) - onehot
    position = jnp.sum(earlier * onehot, axis=1)
    return (flat_ids * capacity + position).astype(jnp.int32)


def swiglu_back(gate_pre, up_pre, grad_hidden):
    sigmoid_gate = jax.nn.sigmoid(gate_pre)
    silu_gate = gate_pre * sigmoid_gate
    hidden = silu_gate * up_pre
    grad_pre_gate = grad_hidden * up_pre * sigmoid_gate * (1.0 + gate_pre * (1.0 - sigmoid_gate))
    grad_pre_up = grad_hidden * silu_gate
    return hidden, grad_pre_gate, grad_pre_up


def reference(tokens, grad_out, probs, expert_ids, w_gate, w_up, w_down):
    block_ids = expert_ids.reshape(EXPERTS, TOK_DEV, TOPK)
    slot_ids = jax.vmap(lambda ids: slot_index(ids, CAP, EXPERTS))(block_ids)
    scaled = (probs[:, :, None] * grad_out.astype(jnp.float32)[:, None, :]).astype(jnp.bfloat16)
    copies_in = jnp.repeat(tokens, TOPK, axis=0).reshape(EXPERTS, TOK_DEV * TOPK, D)
    copies_grad = scaled.reshape(EXPERTS, TOK_DEV * TOPK, D)

    def place_rows(slot_row, copies):
        return jnp.zeros((EXPERTS * CAP, D), copies.dtype).at[slot_row].set(copies)

    def arrange(copies):
        placed = jax.vmap(place_rows)(slot_ids, copies)
        placed = placed.reshape(EXPERTS, EXPERTS, CAP, D).transpose(1, 0, 2, 3)
        return placed.reshape(EXPERTS, ROWS, D)

    expert_in = arrange(copies_in)
    expert_grad = arrange(copies_grad)

    def one_expert(operands):
        rows_in, rows_grad, gate_w, up_w, down_w = operands
        gate_pre = jnp.dot(rows_in, gate_w, preferred_element_type=jnp.float32)
        up_pre = jnp.dot(rows_in, up_w, preferred_element_type=jnp.float32)
        grad_hidden = jnp.dot(rows_grad, down_w.T, preferred_element_type=jnp.float32)
        hidden, grad_pre_gate, grad_pre_up = swiglu_back(gate_pre, up_pre, grad_hidden)
        hidden = hidden.astype(jnp.bfloat16)
        grad_pre_gate = grad_pre_gate.astype(jnp.bfloat16)
        grad_pre_up = grad_pre_up.astype(jnp.bfloat16)
        down_grad = jnp.dot(hidden.T, rows_grad, preferred_element_type=jnp.float32).astype(jnp.bfloat16)
        gate_grad = jnp.dot(rows_in.T, grad_pre_gate, preferred_element_type=jnp.float32).astype(jnp.bfloat16)
        up_grad = jnp.dot(rows_in.T, grad_pre_up, preferred_element_type=jnp.float32).astype(jnp.bfloat16)
        ranges = FF // FF_DEV
        gate_parts = grad_pre_gate.astype(jnp.float32).reshape(ROWS, ranges, FF_DEV)
        up_parts = grad_pre_up.astype(jnp.float32).reshape(ROWS, ranges, FF_DEV)
        gate_rows = gate_w.astype(jnp.float32).reshape(D, ranges, FF_DEV)
        up_rows = up_w.astype(jnp.float32).reshape(D, ranges, FF_DEV)
        partial_value = jnp.einsum("rnf,dnf->rnd", gate_parts, gate_rows) + jnp.einsum("rnf,dnf->rnd", up_parts, up_rows)
        summed = jnp.sum(partial_value.astype(jnp.bfloat16).astype(jnp.float32), axis=1)
        return gate_grad, up_grad, down_grad, summed

    grad_gate, grad_up, grad_down, summed = lax.map(one_expert, (expert_in, expert_grad, w_gate, w_up, w_down))
    back = summed.reshape(EXPERTS, EXPERTS, CAP, D).transpose(1, 0, 2, 3).reshape(EXPERTS, EXPERTS * CAP, D)
    picked = jax.vmap(lambda table, slot_row: table[slot_row])(back, slot_ids)
    grad_tokens = jnp.sum(picked.reshape(TOKENS, TOPK, D), axis=1).astype(jnp.bfloat16)
    return grad_tokens, grad_gate, grad_up, grad_down
```

```python
import jax
import jax.numpy as jnp
from jax import lax
from jax.experimental import pallas as pl
from jax.experimental.pallas import tpu as pltpu
from jax.sharding import PartitionSpec as P

VMEM_LIMIT = 58 * 1024 * 1024
CORES = 2
DEPTH = 4
PAIRS = ((0, 1), (2, 3))
EVEN, ODD = (0, 2), (1, 3)
TILES = 3
COLUMN_PARTS = 6
ELEMENT_COLUMNS = 256
ROUTING_ROWS = 16
ANY = pl.BlockSpec(memory_space=pl.ANY)
VMEM = pl.BlockSpec(memory_space=pltpu.VMEM)
SMEM = pl.BlockSpec(memory_space=pltpu.SMEM)


def product(left, right):
    return jnp.dot(left, right, preferred_element_type=jnp.float32)


def left_product(left, right):
    return lax.dot_general(
        left, right, (((0,), (0,)), ((), ())), preferred_element_type=jnp.float32
    )


def half(*shape):
    return jax.ShapeDtypeStruct(shape, jnp.bfloat16)


def full32(*shape):
    return jax.ShapeDtypeStruct(shape, jnp.float32)


def params():
    return pltpu.CompilerParams(vmem_limit_bytes=VMEM_LIMIT)


def shifted(value, axis, stride, count, step):
    step %= count
    if step == 0:
        return value
    pairs = []
    for src in range(lax.axis_size(axis)):
        place = src // stride % count
        pairs.append((src, src + ((place + step) % count - place) * stride))
    return lax.ppermute(value, axis, pairs)


def whole_call(kernel, args, out_shapes, experts=None, after=()):
    moved = sum(a.size * a.dtype.itemsize for a in args)
    moved += sum(o.size * o.dtype.itemsize for o in out_shapes)
    scalars = [] if experts is None else [experts]
    skipped = len(after)

    def body(*refs):
        kernel(*refs[skipped:])

    return pl.pallas_call(
        body,
        in_specs=[ANY] * skipped + [SMEM] * len(scalars) + [VMEM] * len(args),
        out_specs=[VMEM] * len(out_shapes),
        out_shape=out_shapes,
        compiler_params=params(),
        cost_estimate=pl.CostEstimate(flops=0, bytes_accessed=moved, transcendentals=0),
    )(*after, *scalars, *args)


def pack(tokens, probs, expert_ids):
    tok_rows, width = tokens.shape

    def kernel(t_ref, p_ref, id_ref, out_ref):
        out_ref[:tok_rows, :] = t_ref[...]
        rest = p_ref[...]
        rows = [id_ref[...].astype(jnp.float32)]
        for _ in range(3):
            part = rest.astype(jnp.bfloat16).astype(jnp.float32)
            rows.append(part)
            rest = rest - part
        out_ref[tok_rows:, :] = jnp.zeros((ROUTING_ROWS, width), jnp.bfloat16)
        out_ref[tok_rows:, :tok_rows] = jnp.concatenate(rows, axis=0).astype(jnp.bfloat16)

    assert 4 * probs.shape[0] == ROUTING_ROWS
    return whole_call(
        kernel, [tokens, probs, expert_ids], [half(tok_rows + ROUTING_ROWS, width)]
    )[0]


def routes(ref, tok_rows, expert):
    rows = ref[tok_rows:, :tok_rows].astype(jnp.float32)
    top = ROUTING_ROWS // 4
    hit = rows[:top] == expert.astype(jnp.float32)
    weights = rows[top : 2 * top] + rows[2 * top : 3 * top] + rows[3 * top :]
    prob = jnp.sum(jnp.where(hit, weights, 0.0), axis=0, keepdims=True)
    named = jnp.sum(hit.astype(jnp.float32), axis=0, keepdims=True)
    before = lax.broadcasted_iota(jnp.int32, (tok_rows, tok_rows), 0)
    here = lax.broadcasted_iota(jnp.int32, (tok_rows, tok_rows), 1)
    ahead = (before < here).astype(jnp.float32).astype(jnp.bfloat16)
    many = jnp.broadcast_to(named, (8, tok_rows)).astype(jnp.bfloat16)
    pos = product(many, ahead)[:1]
    return jnp.where(named > 0.0, pos, -1.0).astype(jnp.int32), prob


def hits(pos, capacity):
    slots = lax.broadcasted_iota(jnp.int32, (capacity, pos.shape[1]), 0)
    return slots == pos


def one_hot(pos, capacity):
    return hits(pos, capacity).astype(jnp.float32).astype(jnp.bfloat16)


def pick_rows(even_refs, odd_refs, pick_even, pick_odd, capacity, out_refs):
    keep_ref, even_ref, odd_out = out_refs[0], out_refs[1], out_refs[2:]
    blocks, ranges = len(even_refs), len(odd_refs)
    for dx in range(blocks):
        rows = slice(dx * capacity, (dx + 1) * capacity)
        value = pick_even(dx, even_refs[dx])
        keep_ref[rows, :] = value
        even_ref[rows, :] = value
    for dx in range(blocks):
        for dy in range(ranges):
            value = pick_odd(dx, odd_refs[dy])
            if dx == 0:
                start = (blocks + dy) * capacity
                keep_ref[start : start + capacity, :] = value
            else:
                odd_out[dx - 1][dy * capacity : (dy + 1) * capacity, :] = value


def picked_shapes(blocks, ranges, capacity, width):
    shapes = [half((blocks + ranges) * capacity, width), half(blocks * capacity, width)]
    return shapes + [half(ranges * capacity, width)] * (blocks - 1)


def pick_tokens(experts, even, odd, capacity, after):
    blocks, ranges = len(even), len(odd)
    tok_rows, width = even[0].shape[0] - ROUTING_ROWS, even[0].shape[1]

    def kernel(e_ref, *refs):
        even_refs, refs = refs[:blocks], refs[blocks:]
        odd_refs, refs = refs[:ranges], refs[ranges:]
        pos_ref, prob_ref = refs[-2:]
        for dx in range(blocks):
            pos_ref[0, dx], prob_ref[0, dx] = routes(even_refs[dx], tok_rows, e_ref[0])
            pos_ref[1, dx], prob_ref[1, dx] = routes(odd_refs[0], tok_rows, e_ref[dx])
            pos_ref[2, dx], prob_ref[2, dx] = routes(even_refs[0], tok_rows, e_ref[dx])

        def pick(kind):
            def value(dx, ref):
                chosen = one_hot(pos_ref[kind, dx], capacity)
                return product(chosen, ref[:tok_rows, :]).astype(jnp.bfloat16)

            return value

        pick_rows(even_refs, odd_refs, pick(0), pick(1), capacity, refs[:-2])

    shapes = picked_shapes(blocks, ranges, capacity, width)
    shapes += [jax.ShapeDtypeStruct((3, blocks, 1, tok_rows), jnp.int32)]
    shapes += [full32(3, blocks, 1, tok_rows)]
    outs = whole_call(kernel, [*even, *odd], shapes, experts, after)
    return outs[:-2], outs[-2], outs[-1]


def pick_grads(pos, prob, even, odd, capacity, after):
    blocks, ranges = len(even), len(odd)
    width = even[0].shape[1]

    def kernel(pos_ref, prob_ref, *refs):
        even_refs, refs = refs[:blocks], refs[blocks:]
        odd_refs, out_refs = refs[:ranges], refs[ranges:]

        def pick(kind):
            def value(dx, ref):
                hit = hits(pos_ref[kind, dx], capacity)
                weight = jnp.sum(jnp.where(hit, prob_ref[kind, dx], 0.0), axis=1, keepdims=True)
                chosen = hit.astype(jnp.float32).astype(jnp.bfloat16)
                return (weight * product(chosen, ref[...])).astype(jnp.bfloat16)

            return value

        pick_rows(even_refs, odd_refs, pick(0), pick(1), capacity, out_refs)

    shapes = picked_shapes(blocks, ranges, capacity, width)
    return whole_call(kernel, [pos, prob, *even, *odd], shapes, after=after)


def assemble(x_ref, xt_ref, columns, pieces, refs, blocks, ranges, capacity):
    k_rows = blocks * capacity
    for (pair, kind, d, dc), ref in zip(pieces, refs):
        even_at = pair * k_rows
        odd_at = len(EVEN) * k_rows + pair * capacity
        if kind == "even":
            x_ref[even_at : even_at + k_rows, columns(dc, d)] = ref[...]
        elif kind == "odd":
            start = odd_at + d * len(ODD) * capacity
            for dy in range(ranges):
                x_ref[start : start + capacity, columns(dc, dy)] = ref[
                    dy * capacity : (dy + 1) * capacity, :
                ]
        else:
            x_ref[even_at : even_at + k_rows, columns(dc, 0)] = ref[:k_rows, :]
            for dy in range(ranges):
                x_ref[odd_at : odd_at + capacity, columns(dc, dy)] = ref[
                    k_rows + dy * capacity : k_rows + (dy + 1) * capacity, :
                ]
    part = x_ref.shape[1] // COLUMN_PARTS
    for n in range(COLUMN_PARTS):
        at = slice(n * part, (n + 1) * part)
        xt_ref[at, :] = x_ref[:, at].T


def fixed(a):
    return pl.BlockSpec(a.shape, lambda f, *_: (0,) * a.ndim)


def gate_units(order, names, pieces, weight, blocks, ranges, capacity, after):
    ff, full = weight.shape
    tile, rows, width = ff // TILES, DEPTH * blocks * capacity, pieces[0].shape[1]
    n_in = len(pieces)

    def kernel(order_ref, *refs):
        in_refs, w_ref = refs[:n_in], refs[n_in]
        x_out, xt_out, gate_ref, x_ref, xt_ref, sems = refs[n_in + 1 + len(after) :]
        step = pl.program_id(0)
        saved = [
            pltpu.make_async_copy(x_ref, x_out, sems.at[0]),
            pltpu.make_async_copy(xt_ref, xt_out, sems.at[1]),
        ]

        def columns(dc, dy):
            at = order_ref[dc * ranges + dy] * width
            return pl.ds(pl.multiple_of(at, width), width)

        @pl.when(step == 0)
        def _():
            assemble(x_ref, xt_ref, columns, names, in_refs, blocks, ranges, capacity)
            for copy in saved:
                copy.start()

        gate_ref[...] = product(w_ref[...], xt_ref[...])

        @pl.when(step == TILES - 1)
        def _():
            for copy in saved:
                copy.wait()

    return pl.pallas_call(
        kernel,
        grid_spec=pltpu.PrefetchScalarGridSpec(
            num_scalar_prefetch=1,
            grid=(TILES,),
            in_specs=[fixed(a) for a in pieces]
            + [pl.BlockSpec((tile, full), lambda f, _: (f, 0))]
            + [ANY] * len(after),
            out_specs=[ANY, ANY, pl.BlockSpec((tile, rows), lambda f, _: (f, 0))],
            scratch_shapes=[
                pltpu.VMEM((rows, full), jnp.bfloat16),
                pltpu.VMEM((full, rows), jnp.bfloat16),
                pltpu.SemaphoreType.DMA((2,)),
            ],
        ),
        out_shape=[half(rows, full), half(full, rows), full32(ff, rows)],
        compiler_params=params(),
        cost_estimate=pl.CostEstimate(
            flops=2 * rows * ff * full,
            bytes_accessed=2 * ff * full + 6 * rows * full + 4 * rows * ff,
            transcendentals=0,
        ),
    )(order, *pieces, weight, *after)


def up_units(x_t, weight, after):
    ff, full = weight.shape
    tile, rows = ff // TILES, x_t.shape[1]

    def kernel(w_ref, xt_ref, *refs):
        refs[-1][...] = product(w_ref[...], xt_ref[...])

    return pl.pallas_call(
        kernel,
        grid=(TILES,),
        in_specs=[pl.BlockSpec((tile, full), lambda f: (f, 0)), fixed(x_t)] + [ANY] * len(after),
        out_specs=pl.BlockSpec((tile, rows), lambda f: (f, 0)),
        out_shape=full32(ff, rows),
        compiler_params=params(),
        cost_estimate=pl.CostEstimate(
            flops=2 * rows * ff * full,
            bytes_accessed=2 * ff * full + 2 * rows * full + 4 * rows * ff,
            transcendentals=0,
        ),
    )(weight, x_t, *after)


def hidden_units(order, names, pieces, weight, gate, up, blocks, ranges, capacity, after):
    ff, full = weight.shape
    tile, rows, width = ff // TILES, gate.shape[1], pieces[0].shape[1]
    n_in = len(pieces)

    def kernel(order_ref, *refs):
        in_refs, refs = refs[:n_in], refs[n_in:]
        w_ref, gate_ref, up_ref = refs[:3]
        g_out, hid_ref, gpg_ref, gpu_ref, g_ref, gt_ref, sem = refs[3 + len(after) :]
        step = pl.program_id(0)
        saved = pltpu.make_async_copy(g_ref, g_out, sem)

        def columns(dc, dy):
            at = order_ref[dc * ranges + dy] * width
            return pl.ds(pl.multiple_of(at, width), width)

        @pl.when(step == 0)
        def _():
            assemble(g_ref, gt_ref, columns, names, in_refs, blocks, ranges, capacity)
            saved.start()

        for n in range(0, rows, ELEMENT_COLUMNS):
            at = slice(n, min(n + ELEMENT_COLUMNS, rows))
            grad_hidden = product(w_ref[...], gt_ref[:, at])
            gate_pre, up_pre = gate_ref[:, at], up_ref[:, at]
            sig = jax.nn.sigmoid(gate_pre)
            silu = gate_pre * sig
            hid_ref[:, at] = (silu * up_pre).astype(jnp.bfloat16)
            gpg_ref[:, at] = (
                grad_hidden * up_pre * sig * (1.0 + gate_pre * (1.0 - sig))
            ).astype(jnp.bfloat16)
            gpu_ref[:, at] = (grad_hidden * silu).astype(jnp.bfloat16)

        @pl.when(step == TILES - 1)
        def _():
            saved.wait()

    by_tile = pl.BlockSpec((tile, rows), lambda f, _: (f, 0))
    return pl.pallas_call(
        kernel,
        grid_spec=pltpu.PrefetchScalarGridSpec(
            num_scalar_prefetch=1,
            grid=(TILES,),
            in_specs=[fixed(a) for a in pieces]
            + [pl.BlockSpec((tile, full), lambda f, _: (f, 0)), by_tile, by_tile]
            + [ANY] * len(after),
            out_specs=[ANY, by_tile, by_tile, by_tile],
            scratch_shapes=[
                pltpu.VMEM((rows, full), jnp.bfloat16),
                pltpu.VMEM((full, rows), jnp.bfloat16),
                pltpu.SemaphoreType.DMA,
            ],
        ),
        out_shape=[half(rows, full)] + [half(ff, rows)] * 3,
        compiler_params=params(),
        cost_estimate=pl.CostEstimate(
            flops=2 * rows * ff * full,
            bytes_accessed=2 * ff * full + 4 * rows * full + 14 * rows * ff,
            transcendentals=rows * ff,
        ),
    )(order, *pieces, weight, gate, up, *after)


def partials(order, dc, lefts, weights, ranges, turn, after):
    ff, full = weights[0].shape
    rows = lefts[0].shape[1 if turn else 0]
    width = full // (CORES * ranges)

    def kernel(order_ref, lg_ref, lu_ref, wg_ref, wu_ref, *refs):
        refs = refs[len(after) :]
        if turn:

            @pl.when(pl.program_id(0) == 0)
            def _():
                refs[1][...] = lg_ref[...].T
                refs[2][...] = lu_ref[...].T

            lg_ref, lu_ref = refs[1:]
        value = product(lg_ref[...], wg_ref[...]) + product(lu_ref[...], wu_ref[...])
        refs[0][0] = value.astype(jnp.bfloat16)

    right = pl.BlockSpec((ff, width), lambda r, order: (0, order[dc * ranges + r]))
    turned = pl.BlockSpec((rows, ff), lambda r, _: (0, 0))
    return pl.pallas_call(
        kernel,
        grid_spec=pltpu.PrefetchScalarGridSpec(
            num_scalar_prefetch=1,
            grid=(ranges,),
            in_specs=[fixed(a) for a in lefts] + [right, right] + [ANY] * len(after),
            out_specs=[pl.BlockSpec((1, rows, width), lambda r, _: (r, 0, 0))]
            + [turned] * (2 * turn),
        ),
        out_shape=[half(ranges, rows, width)] + [half(rows, ff)] * (2 * turn),
        compiler_params=params(),
        cost_estimate=pl.CostEstimate(
            flops=4 * rows * ff * full // CORES,
            bytes_accessed=2 * ff * full + 2 * rows * full + 6 * rows * ff,
            transcendentals=0,
        ),
    )(order, *lefts, *weights[:2], *after)


def weight_grad(left, right, after):
    ff, rows = left.shape
    full = right.shape[1]
    part = full // COLUMN_PARTS

    def kernel(left_ref, right_ref, *refs):
        refs[-1][...] = product(left_ref[...], right_ref[...]).astype(jnp.bfloat16)

    return pl.pallas_call(
        kernel,
        grid=(COLUMN_PARTS,),
        in_specs=[fixed(left), pl.BlockSpec((rows, part), lambda n: (0, n))] + [ANY] * len(after),
        out_specs=pl.BlockSpec((ff, part), lambda n: (0, n)),
        out_shape=half(ff, full),
        compiler_params=params(),
        cost_estimate=pl.CostEstimate(
            flops=2 * rows * ff * full,
            bytes_accessed=2 * (rows * ff + full * (ff + rows)),
            transcendentals=0,
        ),
    )(left, right, *after)


def first_returns(own, other, blocks, capacity):
    ranges = own.shape[0]
    evens, odds = len(EVEN) * blocks * capacity, len(ODD) * capacity

    def total(at):
        value = own[at].astype(jnp.float32) + other[at].astype(jnp.float32)
        return value.astype(jnp.bfloat16)

    even = [total((dy, slice(0, evens))) for dy in range(ranges)]
    odd = [
        total((slice(None), slice(evens + dx * odds, evens + (dx + 1) * odds)))
        for dx in range(blocks)
    ]
    return even, odd


def spread(pos, rows):
    return left_product(one_hot(pos, rows.shape[0]), rows)


def second_returns(positions, even, odd, capacity, after):
    ranges, blocks = len(even), len(odd)
    tok_rows, width = positions[0].shape[3], even[0].shape[1]

    def kernel(*refs):
        pos_refs, refs = refs[: len(PAIRS)], refs[len(PAIRS) :]
        even_refs, refs = refs[:ranges], refs[ranges:]
        odd_refs, out_refs = refs[:blocks], refs[blocks:]
        for i in range(len(EVEN)):
            for dx in range(blocks):
                start = (i * blocks + dx) * capacity
                value = even_refs[0][start : start + capacity, :].astype(jnp.float32)
                for dy in range(1, ranges):
                    value += even_refs[dy][start : start + capacity, :].astype(jnp.float32)
                out_refs[dx][i * capacity : (i + 1) * capacity, :] = value.astype(jnp.bfloat16)
        for i in range(len(ODD)):
            rows = slice(i * capacity, (i + 1) * capacity)
            for dy in range(ranges):
                value = spread(pos_refs[i][1, 0], odd_refs[0][dy, rows, :])
                for dx in range(1, blocks):
                    value += spread(pos_refs[i][1, dx], odd_refs[dx][dy, rows, :])
                out_refs[blocks + dy][i * tok_rows : (i + 1) * tok_rows, :] = value.astype(
                    jnp.bfloat16
                )

    shapes = [half(len(EVEN) * capacity, width)] * blocks
    shapes += [half(len(ODD) * tok_rows, width)] * ranges
    outs = whole_call(kernel, [*positions, *even, *odd], shapes, after=after)
    return outs[:blocks], outs[blocks:]


def third_returns(positions, even, odd, capacity, after):
    blocks, ranges = len(even), len(odd)
    tok_rows, width = positions[0].shape[3], even[0].shape[1]

    def kernel(*refs):
        pos_refs, refs = refs[: len(PAIRS)], refs[len(PAIRS) :]
        even_refs, refs = refs[:blocks], refs[blocks:]
        odd_refs, out_refs = refs[:ranges], refs[ranges:]
        for i, k in enumerate(EVEN):
            rows = slice(i * capacity, (i + 1) * capacity)
            value = spread(pos_refs[i][2, 0], even_refs[0][rows, :])
            for dx in range(1, blocks):
                value += spread(pos_refs[i][2, dx], even_refs[dx][rows, :])
            out_refs[k][...] = value.astype(jnp.bfloat16)
        for i, k in enumerate(ODD):
            rows = slice(i * tok_rows, (i + 1) * tok_rows)
            value = odd_refs[0][rows, :].astype(jnp.float32)
            for dy in range(1, ranges):
                value += odd_refs[dy][rows, :].astype(jnp.float32)
            out_refs[k][...] = value.astype(jnp.bfloat16)

    return whole_call(
        kernel, [*positions, *even, *odd], [half(tok_rows, width)] * DEPTH, after=after
    )


def add_up(parts):
    value = parts[0].astype(jnp.float32)
    for part in parts[1:]:
        value += part.astype(jnp.float32)
    return value.astype(jnp.bfloat16)


def ordered(value, after):
    return lax.optimization_barrier((value, tuple(after)))[0] if after else value


def local(tokens, grad_out, probs, expert_ids, w_gate, w_up, w_down):
    experts, etp = lax.axis_size("ep"), lax.axis_size("etp")
    blocks, ranges = experts // DEPTH, etp // CORES
    tok_rows, top_count = expert_ids.shape
    capacity = 3 * tok_rows * top_count // (2 * experts)
    me, mine = lax.axis_index("ep"), lax.axis_index("etp")
    my_z, my_x = me // blocks, me % blocks
    my_y, my_c = mine // CORES, mine % CORES

    def along_z(value, step):
        return shifted(value, "ep", blocks, DEPTH, step)

    def along_x(value, step):
        return shifted(value, "ep", 1, blocks, step)

    def along_y(value, step):
        return shifted(value, "etp", CORES, ranges, step)

    def along_c(value, step):
        return shifted(value, "etp", 1, CORES, step)

    own_experts = jnp.stack([my_z * blocks + (my_x + dx) % blocks for dx in range(blocks)])
    own_experts = own_experts.astype(jnp.int32)
    order = [
        (my_y - dy) % ranges * CORES + (my_c - dc) % CORES
        for dc in range(CORES)
        for dy in range(ranges)
    ]
    order = jnp.stack(order).astype(jnp.int32)
    weights = (w_gate[0].T, w_up[0].T, w_down[0])

    def first_hops(line):
        even = [[along_x(line[k], dx) for dx in range(blocks)] for k in EVEN]
        odd = [[along_y(line[k], dy) for dy in range(ranges)] for k in ODD]
        return list(zip(even, odd))

    def second_hops(outs):
        keep, even, odd = outs[0], outs[1], outs[2:]
        names, arrays = [("keep", 0)], [keep]
        for dy in range(1, ranges):
            names.append(("even", dy))
            arrays.append(along_y(even, dy))
        for dx in range(1, blocks):
            names.append(("odd", dx))
            arrays.append(along_x(odd[dx - 1], dx))
        return names, arrays

    def core_hops(hopped):
        names, arrays = [], []
        for pair, (kinds, values) in enumerate(hopped):
            for (kind, d), value in zip(kinds, values):
                for dc in range(CORES):
                    names.append((pair, kind, d, dc))
                    arrays.append(along_c(value, dc))
        return names, arrays

    packed = pack(tokens, probs.T, expert_ids.T)
    t_line = [along_z(packed, k) for k in range(DEPTH)]
    positions, weightings = [], []

    def picked_tokens(held, after):
        outs, pos, prob = pick_tokens(own_experts, *held, capacity, after)
        positions.append(pos)
        weightings.append(prob)
        return second_hops(outs), (outs[0],)

    t_near, after = picked_tokens(first_hops(t_line)[0], ())
    t_line = [ordered(t, after if k in PAIRS[1] else ()) for k, t in enumerate(t_line)]
    g_line = [grad_out] + [along_z(ordered(grad_out, after), k) for k in range(1, DEPTH)]
    g_near_held = first_hops(g_line)[0]
    after = (*t_near[1][1:], *g_near_held[0][1:], *g_near_held[1][1:])
    t_far, after = picked_tokens(first_hops(t_line)[1], after)
    t_names, t_pieces = core_hops([t_near, t_far])
    after += tuple(t_far[1][1:])
    g_line = [ordered(g, after if k in PAIRS[1] else ()) for k, g in enumerate(g_line)]
    g_first = [g_near_held, first_hops(g_line)[1]]
    sizes = (blocks, ranges, capacity)

    def picked_grads(pair, after):
        outs = pick_grads(positions[pair], weightings[pair], *g_first[pair], capacity, after)
        return second_hops(outs), (outs[0],)

    g_near, after = picked_grads(0, after)
    after += tuple(g_line[k] for k in PAIRS[1])
    x_all, x_t, gate = gate_units(order, t_names, t_pieces, weights[0], *sizes, after)
    g_far, after = picked_grads(1, (gate,))
    up = up_units(x_t, weights[1], after)
    g_names, g_pieces = core_hops([g_near, g_far])
    g_all, hidden, grad_pre_gate, grad_pre_up = hidden_units(
        order, g_names, g_pieces, weights[2], gate, up, *sizes, ()
    )
    other, *lefts = partials(order, 1, (grad_pre_gate, grad_pre_up), weights, ranges, True, ())
    (own,) = partials(order, 0, lefts, weights, ranges, False, ())

    even, odd = first_returns(own, along_c(other, -1), blocks, capacity)
    after = (*even, *odd)
    even = [along_y(a, -dy) for dy, a in enumerate(even)]
    odd = [along_x(a, -dx) for dx, a in enumerate(odd)]
    grad_down = weight_grad(hidden, g_all, after)
    even, odd = second_returns(positions, even, odd, capacity, (grad_down,))
    after = (*even, *odd)
    even = [along_x(a, -dx) for dx, a in enumerate(even)]
    odd = [along_y(a, -dy) for dy, a in enumerate(odd)]
    grad_gate = weight_grad(grad_pre_gate, x_all, after)
    third = third_returns(positions, even, odd, capacity, (grad_gate,))
    grad_up = weight_grad(grad_pre_up, x_all, tuple(third))
    returned = [along_z(a, -k) for k, a in enumerate(third)]
    grad_tokens = add_up(returned)
    return (grad_tokens, grad_gate.T[None], grad_up.T[None], grad_down[None])


def solution(mesh):
    return jax.shard_map(
        local,
        mesh=mesh,
        in_specs=(
            P("ep", "etp"),
            P("ep", "etp"),
            P("ep", None),
            P("ep", None),
            P("ep", None, "etp"),
            P("ep", None, "etp"),
            P("ep", "etp", None),
        ),
        out_specs=(
            P("ep", "etp"),
            P("ep", None, "etp"),
            P("ep", None, "etp"),
            P("ep", "etp", None),
        ),
        check_vma=False,
    )
```

```python
import jax
import jax.numpy as jnp
from jax import lax
from jax.experimental import pallas as pl
from jax.experimental.pallas import tpu as pltpu
from jax.sharding import PartitionSpec as P

VMEM_LIMIT = 58 * 1024 * 1024
CORES = 2
DEPTH = 4
PAIRS = ((0, 1), (2, 3))
TILES = 6
COLUMN_PARTS = 4
ROUTING_ROWS = 16
ANY = pl.BlockSpec(memory_space=pl.ANY)
VMEM = pl.BlockSpec(memory_space=pltpu.VMEM)
SMEM = pl.BlockSpec(memory_space=pltpu.SMEM)


def product(left, right):
    return jnp.dot(left, right, preferred_element_type=jnp.float32)


def left_product(left, right):
    return lax.dot_general(
        left, right, (((0,), (0,)), ((), ())), preferred_element_type=jnp.float32
    )


def half(*shape):
    return jax.ShapeDtypeStruct(shape, jnp.bfloat16)


def right_product(left, right):
    return lax.dot_general(
        left, right, (((1,), (1,)), ((), ())), preferred_element_type=jnp.float32
    )


def full32(*shape):
    return jax.ShapeDtypeStruct(shape, jnp.float32)


def params():
    return pltpu.CompilerParams(vmem_limit_bytes=VMEM_LIMIT)


def shifted(value, axis, stride, count, step):
    step %= count
    if step == 0:
        return value
    pairs = []
    for src in range(lax.axis_size(axis)):
        place = src // stride % count
        pairs.append((src, src + ((place + step) % count - place) * stride))
    return lax.ppermute(value, axis, pairs)


def whole_call(kernel, args, out_shapes, experts=None, after=()):
    scalars = [] if experts is None else [experts]
    skipped = len(after)

    def body(*refs):
        kernel(*refs[skipped:])

    return pl.pallas_call(
        body,
        in_specs=[ANY] * skipped + [SMEM] * len(scalars) + [VMEM] * len(args),
        out_specs=[VMEM] * len(out_shapes),
        out_shape=out_shapes,
        compiler_params=params(),
        cost_estimate=pl.CostEstimate(flops=0, bytes_accessed=1, transcendentals=0),
    )(*after, *scalars, *args)


def pack(tokens, grad_out, probs, expert_ids):
    tok_rows, width = tokens.shape

    def kernel(t_ref, g_ref, p_ref, id_ref, out_ref):
        out_ref[:tok_rows, :] = t_ref[...]
        out_ref[tok_rows : 2 * tok_rows, :] = g_ref[...]
        rest = p_ref[...]
        rows = [id_ref[...].astype(jnp.float32)]
        for _ in range(3):
            part = rest.astype(jnp.bfloat16).astype(jnp.float32)
            rows.append(part)
            rest = rest - part
        out_ref[2 * tok_rows :, :] = jnp.zeros((ROUTING_ROWS, width), jnp.bfloat16)
        out_ref[2 * tok_rows :, :tok_rows] = jnp.concatenate(rows, axis=0).astype(jnp.bfloat16)

    assert 4 * probs.shape[0] == ROUTING_ROWS
    return whole_call(
        kernel, [tokens, grad_out, probs, expert_ids], [half(2 * tok_rows + ROUTING_ROWS, width)]
    )[0]


def routes(ref, tok_rows, expert):
    rows = ref[2 * tok_rows :, :tok_rows].astype(jnp.float32)
    top = ROUTING_ROWS // 4
    hit = rows[:top] == expert.astype(jnp.float32)
    weights = rows[top : 2 * top] + rows[2 * top : 3 * top] + rows[3 * top :]
    prob = jnp.sum(jnp.where(hit, weights, 0.0), axis=0, keepdims=True)
    named = jnp.sum(hit.astype(jnp.float32), axis=0, keepdims=True)
    before = lax.broadcasted_iota(jnp.int32, (tok_rows, tok_rows), 0)
    here = lax.broadcasted_iota(jnp.int32, (tok_rows, tok_rows), 1)
    ahead = (before < here).astype(jnp.float32).astype(jnp.bfloat16)
    many = jnp.broadcast_to(named, (8, tok_rows)).astype(jnp.bfloat16)
    pos = product(many, ahead)[:1]
    return jnp.where(named > 0.0, pos, -1.0).astype(jnp.int32), prob


def hits(pos, capacity):
    slots = lax.broadcasted_iota(jnp.int32, (capacity, pos.shape[1]), 0)
    return slots == pos


def one_hot(pos, capacity):
    return hits(pos, capacity).astype(jnp.float32).astype(jnp.bfloat16)


def pick_pair(experts, even, odd, capacity, after):
    blocks, ranges = len(even), len(odd)
    tok_rows, width = (even[0].shape[0] - ROUTING_ROWS) // 2, even[0].shape[1]

    def kernel(e_ref, *refs):
        even_refs, refs = refs[:blocks], refs[blocks:]
        odd_refs, refs = refs[:ranges], refs[ranges:]
        keep_ref, even_out, odd_out, pos_ref = refs[0], refs[1], refs[2:-1], refs[-1]

        def picked(ref, pos, prob):
            hit = hits(pos, capacity)
            chosen = hit.astype(jnp.float32).astype(jnp.bfloat16)
            weight = jnp.sum(jnp.where(hit, prob, 0.0), axis=1, keepdims=True)
            rows = product(chosen, ref[:tok_rows, :])
            grads = product(chosen, ref[tok_rows : 2 * tok_rows, :])
            return rows.astype(jnp.bfloat16), (weight * grads).astype(jnp.bfloat16)

        for dx in range(blocks):
            pos, prob = routes(even_refs[dx], tok_rows, e_ref[0])
            rows = slice(dx * capacity, (dx + 1) * capacity)
            for i, value in enumerate(picked(even_refs[dx], pos, prob)):
                keep_ref[i, rows, :] = value
                even_out[i, rows, :] = value
            pos_ref[1, dx] = routes(even_refs[0], tok_rows, e_ref[dx])[0]
        for dx in range(blocks):
            pos, prob = routes(odd_refs[0], tok_rows, e_ref[dx])
            pos_ref[0, dx] = pos
            for dy in range(ranges):
                start = (blocks + dy if dx == 0 else dy) * capacity
                out_ref = keep_ref if dx == 0 else odd_out[dx - 1]
                for i, value in enumerate(picked(odd_refs[dy], pos, prob)):
                    out_ref[i, start : start + capacity, :] = value

    shapes = [half(2, (blocks + ranges) * capacity, width), half(2, blocks * capacity, width)]
    shapes += [half(2, ranges * capacity, width)] * (blocks - 1)
    shapes += [jax.ShapeDtypeStruct((2, blocks, 1, tok_rows), jnp.int32)]
    outs = whole_call(kernel, [*even, *odd], shapes, experts, after)
    return outs[:-1], outs[-1]


def fixed(a):
    return pl.BlockSpec(a.shape, lambda f, *_: (0,) * a.ndim)


def hidden_units(chunk, chunks, order, names, pieces, weights, sizes, carried, after):
    ff, full = weights[0].shape
    blocks, ranges, capacity = sizes
    tile, width, k_rows = ff // TILES, pieces[0].shape[2], blocks * capacity
    rows, n_in = 2 * k_rows, len(pieces)

    def kernel(order_ref, *refs):
        in_refs, refs = refs[:n_in], refs[n_in:]
        (wg_ref, wu_ref, wd_ref), refs = refs[:3], refs[3 + len(carried) + len(after) :]
        x_ref, g_ref, hid_ref, gpg_ref, gpu_ref = refs

        def columns(dc, dy):
            at = order_ref[dc * ranges + dy] * width
            return pl.ds(pl.multiple_of(at, width), width)

        def put(out_ref, i):
            for (kind, d, dc), ref in zip(names, in_refs):
                if kind == "even":
                    out_ref[:k_rows, columns(dc, d)] = ref[i]
                    continue
                start = k_rows + d * capacity
                first = k_rows if kind == "keep" else 0
                if kind == "keep":
                    out_ref[:k_rows, columns(dc, 0)] = ref[i, :k_rows, :]
                for dy in range(ranges):
                    at = first + dy * capacity
                    out_ref[start : start + capacity, columns(dc, dy)] = ref[
                        i, at : at + capacity, :
                    ]

        @pl.when(pl.program_id(0) == 0)
        def _():
            put(x_ref, 0)
            put(g_ref, 1)

        gate = right_product(x_ref[...], wg_ref[...])
        up = right_product(x_ref[...], wu_ref[...])
        sig = jax.nn.sigmoid(gate)
        silu = gate * sig
        hid_ref[...] = (silu * up).astype(jnp.bfloat16).T
        slope = up * sig * (1.0 + gate * (1.0 - sig))
        grad_hidden = right_product(g_ref[...], wd_ref[...])
        gpg_ref[...] = (grad_hidden * slope).astype(jnp.bfloat16).T
        gpu_ref[...] = (grad_hidden * silu).astype(jnp.bfloat16).T

    out_shapes = [half(chunks * rows, full)] * 2 + [half(ff, chunks * rows)] * 3
    out_specs = [pl.BlockSpec((rows, full), lambda f, _: (chunk, 0))] * 2
    out_specs += [pl.BlockSpec((tile, rows), lambda f, _: (f, chunk))] * 3
    in_specs = [fixed(a) for a in pieces]
    in_specs += [pl.BlockSpec((tile, full), lambda f, _: (f, 0))] * 3
    first = 1 + len(in_specs)
    in_specs += [ANY] * (len(carried) + len(after))
    return pl.pallas_call(
        kernel,
        grid_spec=pltpu.PrefetchScalarGridSpec(
            num_scalar_prefetch=1, grid=(TILES,), in_specs=in_specs, out_specs=out_specs
        ),
        out_shape=out_shapes,
        input_output_aliases={first + i: i for i in range(len(carried))},
        compiler_params=params(),
        cost_estimate=pl.CostEstimate(
            flops=6 * rows * ff * full,
            bytes_accessed=6 * ff * full + 8 * rows * full + 6 * rows * ff,
            transcendentals=rows * ff,
        ),
    )(order, *pieces, *weights, *carried, *after)


def partials(chunk, chunks, order, lefts, weights, ranges, after):
    ff, full = weights[0].shape
    rows = lefts[0].shape[1] // chunks
    steps = CORES * ranges
    width = full // steps

    def kernel(order_ref, gpg_ref, gpu_ref, wg_ref, wu_ref, *refs):
        own_ref, other_ref, lg_ref, lu_ref = refs[len(after) :]
        step = pl.program_id(0)

        @pl.when(step == 0)
        def _():
            lg_ref[...] = gpg_ref[...].T
            lu_ref[...] = gpu_ref[...].T

        value = product(lg_ref[...], wg_ref[...]) + product(lu_ref[...], wu_ref[...])

        @pl.when(step < ranges)
        def _():
            other_ref[0] = value.astype(jnp.bfloat16)

        @pl.when(step >= ranges)
        def _():
            own_ref[0] = value.astype(jnp.bfloat16)

    left = pl.BlockSpec((ff, rows), lambda r, _: (0, chunk))
    right = pl.BlockSpec((ff, width), lambda r, order: (0, order[lax.rem(r + ranges, steps)]))
    own = pl.BlockSpec((1, rows, width), lambda r, _: (jnp.maximum(r - ranges, 0), 0, 0))
    other = pl.BlockSpec((1, rows, width), lambda r, _: (jnp.minimum(r, ranges - 1), 0, 0))
    return pl.pallas_call(
        kernel,
        grid_spec=pltpu.PrefetchScalarGridSpec(
            num_scalar_prefetch=1,
            grid=(steps,),
            in_specs=[left, left, right, right] + [ANY] * len(after),
            out_specs=[own, other],
            scratch_shapes=[pltpu.VMEM((rows, ff), jnp.bfloat16)] * 2,
        ),
        out_shape=[half(ranges, rows, width)] * 2,
        compiler_params=params(),
        cost_estimate=pl.CostEstimate(
            flops=4 * rows * ff * full,
            bytes_accessed=4 * ff * full + 2 * rows * full + 4 * rows * ff,
            transcendentals=0,
        ),
    )(order, *lefts, *weights[:2], *after)


def weight_grad(left, right, parts, held, after):
    ff, rows = left.shape
    full = right.shape[1]
    part = full // COLUMN_PARTS
    start, stop = parts

    def kernel(left_ref, right_ref, *refs):
        refs[-1][...] = product(left_ref[...], right_ref[...]).astype(jnp.bfloat16)

    return pl.pallas_call(
        kernel,
        grid=(stop - start,),
        in_specs=[fixed(left), pl.BlockSpec((rows, part), lambda n: (0, start + n))]
        + [ANY] * (len(held) + len(after)),
        out_specs=pl.BlockSpec((ff, part), lambda n: (0, start + n)),
        out_shape=half(ff, full),
        input_output_aliases={2: 0} if held else {},
        compiler_params=params(),
        cost_estimate=pl.CostEstimate(
            flops=2 * rows * ff * part * (stop - start),
            bytes_accessed=2 * (rows * ff + part * (stop - start) * (ff + rows)),
            transcendentals=0,
        ),
    )(left, right, *held, *after)


def first_returns(own, other, sizes):
    blocks, ranges, capacity = sizes

    def total(at):
        value = own[at].astype(jnp.float32) + other[at].astype(jnp.float32)
        return value.astype(jnp.bfloat16)

    k_rows = blocks * capacity
    even = [total((dy, slice(0, k_rows))) for dy in range(ranges)]
    starts = [k_rows + dx * capacity for dx in range(blocks)]
    return even, [total((slice(None), slice(at, at + capacity))) for at in starts]


def spread(pos, rows):
    chosen = hits(pos, rows.shape[0]).astype(jnp.float32).astype(jnp.bfloat16)
    return left_product(chosen, rows)


def second_returns(pos, even, odd, after):
    ranges, blocks = len(even), len(odd)
    tok_rows, width = pos.shape[3], even[0].shape[1]
    capacity = even[0].shape[0] // blocks

    def kernel(pos_ref, *refs):
        even_refs, refs = refs[:ranges], refs[ranges:]
        odd_refs, out_refs = refs[:blocks], refs[blocks:]
        for dx in range(blocks):
            rows = slice(dx * capacity, (dx + 1) * capacity)
            value = even_refs[0][rows, :].astype(jnp.float32)
            for dy in range(1, ranges):
                value += even_refs[dy][rows, :].astype(jnp.float32)
            out_refs[dx][...] = value.astype(jnp.bfloat16)
        for dy in range(ranges):
            value = spread(pos_ref[0, 0], odd_refs[0][dy])
            for dx in range(1, blocks):
                value += spread(pos_ref[0, dx], odd_refs[dx][dy])
            out_refs[blocks + dy][...] = value.astype(jnp.bfloat16)

    shapes = [half(capacity, width)] * blocks + [half(tok_rows, width)] * ranges
    outs = whole_call(kernel, [pos, *even, *odd], shapes, after=after)
    return outs[:blocks], outs[blocks:]


def third_returns(pos, even, odd, after):
    blocks, ranges = len(even), len(odd)
    tok_rows, width = pos.shape[3], even[0].shape[1]

    def kernel(pos_ref, *refs):
        even_refs, refs = refs[:blocks], refs[blocks:]
        odd_refs, out_refs = refs[:ranges], refs[ranges:]
        value = spread(pos_ref[1, 0], even_refs[0][...])
        for dx in range(1, blocks):
            value += spread(pos_ref[1, dx], even_refs[dx][...])
        out_refs[0][...] = value.astype(jnp.bfloat16)
        value = odd_refs[0][...].astype(jnp.float32)
        for dy in range(1, ranges):
            value += odd_refs[dy][...].astype(jnp.float32)
        out_refs[1][...] = value.astype(jnp.bfloat16)

    return whole_call(kernel, [pos, *even, *odd], [half(tok_rows, width)] * 2, after=after)


def add_up(parts):
    value = parts[0].astype(jnp.float32)
    for part in parts[1:]:
        value += part.astype(jnp.float32)
    return value.astype(jnp.bfloat16)


def ordered(value, after):
    return lax.optimization_barrier((value, tuple(after)))[0] if after else value


def local(tokens, grad_out, probs, expert_ids, w_gate, w_up, w_down):
    experts, etp = lax.axis_size("ep"), lax.axis_size("etp")
    blocks, ranges = experts // DEPTH, etp // CORES
    tok_rows, top_count = expert_ids.shape
    capacity = 3 * tok_rows * top_count // (2 * experts)
    me, mine = lax.axis_index("ep"), lax.axis_index("etp")
    my_z, my_x = me // blocks, me % blocks
    my_y, my_c = mine // CORES, mine % CORES

    def along_z(value, step):
        return shifted(value, "ep", blocks, DEPTH, step)

    def along_x(value, step):
        return shifted(value, "ep", 1, blocks, step)

    def along_y(value, step):
        return shifted(value, "etp", CORES, ranges, step)

    def along_c(value, step):
        return shifted(value, "etp", 1, CORES, step)

    own_experts = jnp.stack([my_z * blocks + (my_x + dx) % blocks for dx in range(blocks)])
    own_experts = own_experts.astype(jnp.int32)
    order = [
        (my_y - dy) % ranges * CORES + (my_c - dc) % CORES
        for dc in range(CORES)
        for dy in range(ranges)
    ]
    order = jnp.stack(order).astype(jnp.int32)
    weights = (w_gate[0].T, w_up[0].T, w_down[0])

    def first_hops(line):
        even = [[along_x(line[k], dx) for dx in range(blocks)] for k in EVEN]
        odd = [[along_y(line[k], dy) for dy in range(ranges)] for k in ODD]
        return list(zip(even, odd))

    def second_hops(outs):
        keep, even, odd = outs[0], outs[1], outs[2:]
        names, arrays = [("keep", 0)], [keep]
        for dy in range(1, ranges):
            names.append(("even", dy))
            arrays.append(along_y(even, dy))
        for dx in range(1, blocks):
            names.append(("odd", dx))
            arrays.append(along_x(odd[dx - 1], dx))
        return names, arrays

    def core_hops(hopped):
        names, arrays = [], []
        for pair, (kinds, values) in enumerate(hopped):
            for (kind, d), value in zip(kinds, values):
                for dc in range(CORES):
                    names.append((pair, kind, d, dc))
                    arrays.append(along_c(value, dc))
        return names, arrays

    sizes = (blocks, ranges, capacity)
    packed = pack(tokens, grad_out, probs.T, expert_ids.T)
    line = [along_z(packed, k) for k in range(DEPTH)]

    def first_hops(pair):
        even = [along_x(line[pair[0]], dx) for dx in range(blocks)]
        return even, [along_y(line[pair[1]], dy) for dy in range(ranges)]

    def gathered(even, odd, after):
        outs, pos = pick_pair(own_experts, even, odd, capacity, after)
        names, arrays = [("keep", 0)], [outs[0]]
        for dy in range(1, ranges):
            names.append(("even", dy))
            arrays.append(along_y(outs[1], dy))
        for dx in range(1, blocks):
            names.append(("odd", dx))
            arrays.append(along_x(outs[1 + dx], dx))
        return pos, names, arrays

    def units(chunk, names, arrays, carried, after):
        names = [(kind, d, dc) for kind, d in names for dc in range(CORES)]
        pieces = [along_c(a, dc) for a in arrays for dc in range(CORES)]
        return hidden_units(
            chunk, len(PAIRS), order, names, pieces, weights, sizes, carried, after
        )

    def sums(chunk, carried, after):
        return partials(chunk, len(PAIRS), order, carried[3:], weights, ranges, after)

    def first_step(parts, after):
        own, other = ordered((parts[0], along_c(parts[1], -1)), after)
        even, odd = first_returns(own, other, sizes)
        arrived = [along_y(a, -dy) for dy, a in enumerate(even)]
        return (*even, *odd), arrived, [along_x(a, -dx) for dx, a in enumerate(odd)]

    def second_step(pos, even, odd, after):
        even, odd = second_returns(pos, even, odd, after)
        arrived = [along_x(a, -dx) for dx, a in enumerate(even)]
        return (*even, *odd), arrived, [along_y(a, -dy) for dy, a in enumerate(odd)]

    def third_step(pair, pos, even, odd, after):
        outs = third_returns(pos, even, odd, after)
        return tuple(outs), [along_z(a, -k) for k, a in zip(pair, outs)]

    pos_a, names, arrays_a = gathered(*first_hops(PAIRS[0]), ())
    even_b, odd_b = first_hops(PAIRS[1])
    pos_b, names, arrays_b = gathered(even_b, odd_b, tuple(arrays_a))
    arrays_a = [arrays_a[0], *ordered(tuple(arrays_a[1:]), (*even_b[1:], *odd_b[1:]))]
    carried = units(0, names, arrays_a, [], (arrays_b[0],))
    arrays_b = [arrays_b[0], *ordered(tuple(arrays_b[1:]), (carried[2],))]
    parts_a = sums(0, carried, tuple(arrays_b[1:]))
    carried = units(1, names, arrays_b, carried, (parts_a[0],))
    done, even_a, odd_a = first_step(parts_a, (carried[2],))
    parts_b = sums(1, carried, done)
    x_all, g_all, hidden, grad_pre_gate, grad_pre_up = carried
    done, even_a, odd_a = second_step(pos_a, even_a, odd_a, (parts_b[0],))
    middle, end = COLUMN_PARTS // 2, COLUMN_PARTS
    grad_down = weight_grad(hidden, g_all, (0, middle), [], done)
    done_a, returned_a = third_step(PAIRS[0], pos_a, even_a, odd_a, (grad_down,))
    done, even_b, odd_b = first_step(parts_b, (grad_down,))
    grad_down = weight_grad(hidden, g_all, (middle, end), [grad_down], done_a + done)
    done, even_b, odd_b = second_step(pos_b, even_b, odd_b, (grad_down,))
    grad_gate = weight_grad(grad_pre_gate, x_all, (0, end), [], done)
    done, returned_b = third_step(PAIRS[1], pos_b, even_b, odd_b, (grad_gate,))
    grad_up = weight_grad(grad_pre_up, x_all, (0, end), [], done)
    grad_tokens = add_up(returned_a + returned_b)
    return (grad_tokens, grad_gate.T[None], grad_up.T[None], grad_down[None])


def solution(mesh):
    return jax.shard_map(
        local,
        mesh=mesh,
        in_specs=(
            P("ep", "etp"),
            P("ep", "etp"),
            P("ep", None),
            P("ep", None),
            P("ep", None, "etp"),
            P("ep", None, "etp"),
            P("ep", "etp", None),
        ),
        out_specs=(
            P("ep", "etp"),
            P("ep", None, "etp"),
            P("ep", None, "etp"),
            P("ep", "etp", None),
        ),
        check_vma=False,
    )
```

```python
import jax
import jax.numpy as jnp
from jax import lax
from jax.experimental import pallas as pl
from jax.experimental.pallas import tpu as pltpu
from jax.sharding import PartitionSpec as P

VMEM_LIMIT = 58 * 1024 * 1024
CORES = 2
DEPTH = 4
PAIRS = ((0, 1), (2, 3))
TILES = 6
ROUTING_ROWS = 16
ANY = pl.BlockSpec(memory_space=pl.ANY)
VMEM = pl.BlockSpec(memory_space=pltpu.VMEM)
SMEM = pl.BlockSpec(memory_space=pltpu.SMEM)


def product(left, right):
    return jnp.dot(left, right, preferred_element_type=jnp.float32)


def left_product(left, right):
    return lax.dot_general(
        left, right, (((0,), (0,)), ((), ())), preferred_element_type=jnp.float32
    )


def half(*shape):
    return jax.ShapeDtypeStruct(shape, jnp.bfloat16)


def right_product(left, right):
    return lax.dot_general(
        left, right, (((1,), (1,)), ((), ())), preferred_element_type=jnp.float32
    )


def full32(*shape):
    return jax.ShapeDtypeStruct(shape, jnp.float32)


def params():
    return pltpu.CompilerParams(vmem_limit_bytes=VMEM_LIMIT)


def shifted(value, axis, stride, count, step):
    step %= count
    if step == 0:
        return value
    pairs = []
    for src in range(lax.axis_size(axis)):
        place = src // stride % count
        pairs.append((src, src + ((place + step) % count - place) * stride))
    return lax.ppermute(value, axis, pairs)


def whole_call(kernel, args, out_shapes, experts=None, after=()):
    scalars = [] if experts is None else [experts]
    skipped = len(after)

    def body(*refs):
        kernel(*refs[skipped:])

    return pl.pallas_call(
        body,
        in_specs=[ANY] * skipped + [SMEM] * len(scalars) + [VMEM] * len(args),
        out_specs=[VMEM] * len(out_shapes),
        out_shape=out_shapes,
        compiler_params=params(),
        cost_estimate=pl.CostEstimate(flops=0, bytes_accessed=1, transcendentals=0),
    )(*after, *scalars, *args)


def pack(tokens, grad_out, probs, expert_ids):
    tok_rows, width = tokens.shape

    def kernel(t_ref, g_ref, p_ref, id_ref, out_ref):
        out_ref[:tok_rows, :] = t_ref[...]
        out_ref[tok_rows : 2 * tok_rows, :] = g_ref[...]
        rest = p_ref[...]
        rows = [id_ref[...].astype(jnp.float32)]
        for _ in range(3):
            part = rest.astype(jnp.bfloat16).astype(jnp.float32)
            rows.append(part)
            rest = rest - part
        out_ref[2 * tok_rows :, :] = jnp.zeros((ROUTING_ROWS, width), jnp.bfloat16)
        out_ref[2 * tok_rows :, :tok_rows] = jnp.concatenate(rows, axis=0).astype(jnp.bfloat16)

    assert 4 * probs.shape[0] == ROUTING_ROWS
    return whole_call(
        kernel, [tokens, grad_out, probs, expert_ids], [half(2 * tok_rows + ROUTING_ROWS, width)]
    )[0]


def routes(ref, tok_rows, expert):
    rows = ref[2 * tok_rows :, :tok_rows].astype(jnp.float32)
    top = ROUTING_ROWS // 4
    hit = rows[:top] == expert.astype(jnp.float32)
    weights = rows[top : 2 * top] + rows[2 * top : 3 * top] + rows[3 * top :]
    prob = jnp.sum(jnp.where(hit, weights, 0.0), axis=0, keepdims=True)
    named = jnp.sum(hit.astype(jnp.float32), axis=0, keepdims=True)
    before = lax.broadcasted_iota(jnp.int32, (tok_rows, tok_rows), 0)
    here = lax.broadcasted_iota(jnp.int32, (tok_rows, tok_rows), 1)
    ahead = (before < here).astype(jnp.float32).astype(jnp.bfloat16)
    many = jnp.broadcast_to(named, (8, tok_rows)).astype(jnp.bfloat16)
    pos = product(many, ahead)[:1]
    return jnp.where(named > 0.0, pos, -1.0).astype(jnp.int32), prob


def hits(pos, capacity):
    slots = lax.broadcasted_iota(jnp.int32, (capacity, pos.shape[1]), 0)
    return slots == pos


def one_hot(pos, capacity):
    return hits(pos, capacity).astype(jnp.float32).astype(jnp.bfloat16)


def pick_pair(experts, even, odd, capacity, after):
    blocks, ranges = len(even), len(odd)
    tok_rows, width = (even[0].shape[0] - ROUTING_ROWS) // 2, even[0].shape[1]

    def kernel(e_ref, *refs):
        even_refs, refs = refs[:blocks], refs[blocks:]
        odd_refs, refs = refs[:ranges], refs[ranges:]
        keep_ref, even_out, odd_out, pos_ref = refs[0], refs[1], refs[2:-1], refs[-1]

        def picked(ref, pos, prob):
            hit = hits(pos, capacity)
            chosen = hit.astype(jnp.float32).astype(jnp.bfloat16)
            weight = jnp.sum(jnp.where(hit, prob, 0.0), axis=1, keepdims=True)
            rows = product(chosen, ref[:tok_rows, :])
            grads = product(chosen, ref[tok_rows : 2 * tok_rows, :])
            return rows.astype(jnp.bfloat16), (weight * grads).astype(jnp.bfloat16)

        for dx in range(blocks):
            pos, prob = routes(even_refs[dx], tok_rows, e_ref[0])
            rows = slice(dx * capacity, (dx + 1) * capacity)
            for i, value in enumerate(picked(even_refs[dx], pos, prob)):
                keep_ref[i, rows, :] = value
                even_out[i, rows, :] = value
            pos_ref[1, dx] = routes(even_refs[0], tok_rows, e_ref[dx])[0]
        for dx in range(blocks):
            pos, prob = routes(odd_refs[0], tok_rows, e_ref[dx])
            pos_ref[0, dx] = pos
            for dy in range(ranges):
                start = (blocks + dy if dx == 0 else dy) * capacity
                out_ref = keep_ref if dx == 0 else odd_out[dx - 1]
                for i, value in enumerate(picked(odd_refs[dy], pos, prob)):
                    out_ref[i, start : start + capacity, :] = value

    shapes = [half(2, (blocks + ranges) * capacity, width), half(2, blocks * capacity, width)]
    shapes += [half(2, ranges * capacity, width)] * (blocks - 1)
    shapes += [jax.ShapeDtypeStruct((2, blocks, 1, tok_rows), jnp.int32)]
    outs = whole_call(kernel, [*even, *odd], shapes, experts, after)
    return outs[:-1], outs[-1]


def fixed(a):
    return pl.BlockSpec(a.shape, lambda f, *_: (0,) * a.ndim)


def hidden_units(chunk, chunks, order, names, pieces, weights, sizes, carried, after):
    ff, full = weights[0].shape
    blocks, ranges, capacity = sizes
    tile, width, k_rows = ff // TILES, pieces[0].shape[2], blocks * capacity
    rows, n_in = 2 * k_rows, len(pieces)

    def kernel(order_ref, *refs):
        in_refs, refs = refs[:n_in], refs[n_in:]
        (wg_ref, wu_ref, wd_ref), refs = refs[:3], refs[3 + len(carried) + len(after) :]
        x_ref, g_ref, hid_ref, gpg_ref, gpu_ref = refs

        def columns(dc, dy):
            at = order_ref[dc * ranges + dy] * width
            return pl.ds(pl.multiple_of(at, width), width)

        def put(out_ref, i):
            for (kind, d, dc), ref in zip(names, in_refs):
                if kind == "even":
                    out_ref[:k_rows, columns(dc, d)] = ref[i]
                    continue
                start = k_rows + d * capacity
                first = k_rows if kind == "keep" else 0
                if kind == "keep":
                    out_ref[:k_rows, columns(dc, 0)] = ref[i, :k_rows, :]
                for dy in range(ranges):
                    at = first + dy * capacity
                    out_ref[start : start + capacity, columns(dc, dy)] = ref[
                        i, at : at + capacity, :
                    ]

        @pl.when(pl.program_id(0) == 0)
        def _():
            put(x_ref, 0)
            put(g_ref, 1)

        gate = right_product(x_ref[...], wg_ref[...])
        up = right_product(x_ref[...], wu_ref[...])
        sig = jax.nn.sigmoid(gate)
        silu = gate * sig
        hid_ref[...] = (silu * up).astype(jnp.bfloat16).T
        slope = up * sig * (1.0 + gate * (1.0 - sig))
        grad_hidden = right_product(g_ref[...], wd_ref[...])
        gpg_ref[...] = (grad_hidden * slope).astype(jnp.bfloat16).T
        gpu_ref[...] = (grad_hidden * silu).astype(jnp.bfloat16).T

    out_shapes = [half(chunks * rows, full)] * 2 + [half(ff, chunks * rows)] * 3
    out_specs = [pl.BlockSpec((rows, full), lambda f, _: (chunk, 0))] * 2
    out_specs += [pl.BlockSpec((tile, rows), lambda f, _: (f, chunk))] * 3
    in_specs = [fixed(a) for a in pieces]
    in_specs += [pl.BlockSpec((tile, full), lambda f, _: (f, 0))] * 3
    first = 1 + len(in_specs)
    in_specs += [ANY] * (len(carried) + len(after))
    return pl.pallas_call(
        kernel,
        grid_spec=pltpu.PrefetchScalarGridSpec(
            num_scalar_prefetch=1, grid=(TILES,), in_specs=in_specs, out_specs=out_specs
        ),
        out_shape=out_shapes,
        input_output_aliases={first + i: i for i in range(len(carried))},
        compiler_params=params(),
        cost_estimate=pl.CostEstimate(
            flops=6 * rows * ff * full,
            bytes_accessed=6 * ff * full + 8 * rows * full + 6 * rows * ff,
            transcendentals=rows * ff,
        ),
    )(order, *pieces, *weights, *carried, *after)


def partials(chunk, chunks, order, lefts, weights, ranges, after):
    ff, full = weights[0].shape
    rows = lefts[0].shape[1] // chunks
    steps = CORES * ranges
    width = full // steps

    def kernel(order_ref, gpg_ref, gpu_ref, wg_ref, wu_ref, *refs):
        own_ref, other_ref, lg_ref, lu_ref = refs[len(after) :]
        step = pl.program_id(0)

        @pl.when(step == 0)
        def _():
            lg_ref[...] = gpg_ref[...].T
            lu_ref[...] = gpu_ref[...].T

        value = product(lg_ref[...], wg_ref[...]) + product(lu_ref[...], wu_ref[...])

        @pl.when(step < ranges)
        def _():
            other_ref[0] = value.astype(jnp.bfloat16)

        @pl.when(step >= ranges)
        def _():
            own_ref[0] = value.astype(jnp.bfloat16)

    left = pl.BlockSpec((ff, rows), lambda r, _: (0, chunk))
    right = pl.BlockSpec((ff, width), lambda r, order: (0, order[lax.rem(r + ranges, steps)]))
    own = pl.BlockSpec((1, rows, width), lambda r, _: (jnp.maximum(r - ranges, 0), 0, 0))
    other = pl.BlockSpec((1, rows, width), lambda r, _: (jnp.minimum(r, ranges - 1), 0, 0))
    return pl.pallas_call(
        kernel,
        grid_spec=pltpu.PrefetchScalarGridSpec(
            num_scalar_prefetch=1,
            grid=(steps,),
            in_specs=[left, left, right, right] + [ANY] * len(after),
            out_specs=[own, other],
            scratch_shapes=[pltpu.VMEM((rows, ff), jnp.bfloat16)] * 2,
        ),
        out_shape=[half(ranges, rows, width)] * 2,
        compiler_params=params(),
        cost_estimate=pl.CostEstimate(
            flops=4 * rows * ff * full,
            bytes_accessed=4 * ff * full + 2 * rows * full + 4 * rows * ff,
            transcendentals=0,
        ),
    )(order, *lefts, *weights[:2], *after)


def partials_of_core(chunk, chunks, order, dc, lefts, weights, ranges, turn, after):
    ff, full = weights[0].shape
    rows = lefts[0].shape[1] // chunks if turn else lefts[0].shape[0]
    width = full // (CORES * ranges)

    def kernel(order_ref, lg_ref, lu_ref, wg_ref, wu_ref, *refs):
        refs = refs[len(after) :]
        if turn:

            @pl.when(pl.program_id(0) == 0)
            def _():
                refs[1][...] = lg_ref[...].T
                refs[2][...] = lu_ref[...].T

            lg_ref, lu_ref = refs[1:]
        value = product(lg_ref[...], wg_ref[...]) + product(lu_ref[...], wu_ref[...])
        refs[0][0] = value.astype(jnp.bfloat16)

    right = pl.BlockSpec((ff, width), lambda r, order: (0, order[dc * ranges + r]))
    turned = pl.BlockSpec((rows, ff), lambda r, _: (0, 0))
    left = pl.BlockSpec((ff, rows), lambda r, _: (0, chunk)) if turn else turned
    return pl.pallas_call(
        kernel,
        grid_spec=pltpu.PrefetchScalarGridSpec(
            num_scalar_prefetch=1,
            grid=(ranges,),
            in_specs=[left, left, right, right] + [ANY] * len(after),
            out_specs=[pl.BlockSpec((1, rows, width), lambda r, _: (r, 0, 0))]
            + [turned] * (2 * turn),
        ),
        out_shape=[half(ranges, rows, width)] + [half(rows, ff)] * (2 * turn),
        compiler_params=params(),
        cost_estimate=pl.CostEstimate(
            flops=4 * rows * ff * full // CORES,
            bytes_accessed=2 * ff * full + rows * full + 4 * rows * ff,
            transcendentals=0,
        ),
    )(order, *lefts, *weights[:2], *after)


def weight_grad(left, right, after):
    return product(ordered(left, after), right).astype(jnp.bfloat16)


def first_returns(own, other, sizes):
    blocks, ranges, capacity = sizes

    def total(at):
        value = own[at].astype(jnp.float32) + other[at].astype(jnp.float32)
        return value.astype(jnp.bfloat16)

    k_rows = blocks * capacity
    even = [total((dy, slice(0, k_rows))) for dy in range(ranges)]
    starts = [k_rows + dx * capacity for dx in range(blocks)]
    return even, [total((slice(None), slice(at, at + capacity))) for at in starts]


def spread(pos, rows):
    chosen = hits(pos, rows.shape[0]).astype(jnp.float32).astype(jnp.bfloat16)
    return left_product(chosen, rows)


def second_returns(pos, even, odd, after):
    ranges, blocks = len(even), len(odd)
    tok_rows, width = pos.shape[3], even[0].shape[1]
    capacity = even[0].shape[0] // blocks

    def kernel(pos_ref, *refs):
        even_refs, refs = refs[:ranges], refs[ranges:]
        odd_refs, out_refs = refs[:blocks], refs[blocks:]
        for dx in range(blocks):
            rows = slice(dx * capacity, (dx + 1) * capacity)
            value = even_refs[0][rows, :].astype(jnp.float32)
            for dy in range(1, ranges):
                value += even_refs[dy][rows, :].astype(jnp.float32)
            out_refs[dx][...] = value.astype(jnp.bfloat16)
        for dy in range(ranges):
            value = spread(pos_ref[0, 0], odd_refs[0][dy])
            for dx in range(1, blocks):
                value += spread(pos_ref[0, dx], odd_refs[dx][dy])
            out_refs[blocks + dy][...] = value.astype(jnp.bfloat16)

    shapes = [half(capacity, width)] * blocks + [half(tok_rows, width)] * ranges
    outs = whole_call(kernel, [pos, *even, *odd], shapes, after=after)
    return outs[:blocks], outs[blocks:]


def third_returns(pos, even, odd, after):
    blocks, ranges = len(even), len(odd)
    tok_rows, width = pos.shape[3], even[0].shape[1]

    def kernel(pos_ref, *refs):
        even_refs, refs = refs[:blocks], refs[blocks:]
        odd_refs, out_refs = refs[:ranges], refs[ranges:]
        value = spread(pos_ref[1, 0], even_refs[0][...])
        for dx in range(1, blocks):
            value += spread(pos_ref[1, dx], even_refs[dx][...])
        out_refs[0][...] = value.astype(jnp.bfloat16)
        value = odd_refs[0][...].astype(jnp.float32)
        for dy in range(1, ranges):
            value += odd_refs[dy][...].astype(jnp.float32)
        out_refs[1][...] = value.astype(jnp.bfloat16)

    return whole_call(kernel, [pos, *even, *odd], [half(tok_rows, width)] * 2, after=after)


def add_up(parts):
    value = parts[0].astype(jnp.float32)
    for part in parts[1:]:
        value += part.astype(jnp.float32)
    return value.astype(jnp.bfloat16)


def ordered(value, after):
    return lax.optimization_barrier((value, tuple(after)))[0] if after else value


def local(tokens, grad_out, probs, expert_ids, w_gate, w_up, w_down):
    experts, etp = lax.axis_size("ep"), lax.axis_size("etp")
    blocks, ranges = experts // DEPTH, etp // CORES
    tok_rows, top_count = expert_ids.shape
    capacity = 3 * tok_rows * top_count // (2 * experts)
    me, mine = lax.axis_index("ep"), lax.axis_index("etp")
    my_z, my_x = me // blocks, me % blocks
    my_y, my_c = mine // CORES, mine % CORES

    def along_z(value, step):
        return shifted(value, "ep", blocks, DEPTH, step)

    def along_x(value, step):
        return shifted(value, "ep", 1, blocks, step)

    def along_y(value, step):
        return shifted(value, "etp", CORES, ranges, step)

    def along_c(value, step):
        return shifted(value, "etp", 1, CORES, step)

    own_experts = jnp.stack([my_z * blocks + (my_x + dx) % blocks for dx in range(blocks)])
    own_experts = own_experts.astype(jnp.int32)
    order = [
        (my_y - dy) % ranges * CORES + (my_c - dc) % CORES
        for dc in range(CORES)
        for dy in range(ranges)
    ]
    order = jnp.stack(order).astype(jnp.int32)
    weights = (w_gate[0].T, w_up[0].T, w_down[0])

    def first_hops(line):
        even = [[along_x(line[k], dx) for dx in range(blocks)] for k in EVEN]
        odd = [[along_y(line[k], dy) for dy in range(ranges)] for k in ODD]
        return list(zip(even, odd))

    def second_hops(outs):
        keep, even, odd = outs[0], outs[1], outs[2:]
        names, arrays = [("keep", 0)], [keep]
        for dy in range(1, ranges):
            names.append(("even", dy))
            arrays.append(along_y(even, dy))
        for dx in range(1, blocks):
            names.append(("odd", dx))
            arrays.append(along_x(odd[dx - 1], dx))
        return names, arrays

    def core_hops(hopped):
        names, arrays = [], []
        for pair, (kinds, values) in enumerate(hopped):
            for (kind, d), value in zip(kinds, values):
                for dc in range(CORES):
                    names.append((pair, kind, d, dc))
                    arrays.append(along_c(value, dc))
        return names, arrays

    sizes = (blocks, ranges, capacity)
    packed = pack(tokens, grad_out, probs.T, expert_ids.T)
    line = [along_z(packed, k) for k in range(DEPTH)]

    def first_hops(pair):
        even = [along_x(line[pair[0]], dx) for dx in range(blocks)]
        return even, [along_y(line[pair[1]], dy) for dy in range(ranges)]

    def gathered(even, odd, after):
        outs, pos = pick_pair(own_experts, even, odd, capacity, after)
        names, arrays = [("keep", 0)], [outs[0]]
        for dy in range(1, ranges):
            names.append(("even", dy))
            arrays.append(along_y(outs[1], dy))
        for dx in range(1, blocks):
            names.append(("odd", dx))
            arrays.append(along_x(outs[1 + dx], dx))
        return pos, names, arrays

    def units(chunk, names, arrays, carried, after):
        names = [(kind, d, dc) for kind, d in names for dc in range(CORES)]
        pieces = [along_c(a, dc) for a in arrays for dc in range(CORES)]
        return hidden_units(
            chunk, len(PAIRS), order, names, pieces, weights, sizes, carried, after
        )

    def sums(chunk, carried, after):
        return partials(chunk, len(PAIRS), order, carried[3:], weights, ranges, after)

    def first_step(own, other, after):
        even, odd = first_returns(*ordered((own, other), after), sizes)
        arrived = [along_y(a, -dy) for dy, a in enumerate(even)]
        return (*even, *odd), arrived, [along_x(a, -dx) for dx, a in enumerate(odd)]

    def second_step(pos, even, odd, after):
        even, odd = second_returns(pos, even, odd, after)
        arrived = [along_x(a, -dx) for dx, a in enumerate(even)]
        return (*even, *odd), arrived, [along_y(a, -dy) for dy, a in enumerate(odd)]

    def third_step(pair, pos, even, odd, after):
        outs = third_returns(pos, even, odd, after)
        return tuple(outs), [along_z(a, -k) for k, a in zip(pair, outs)]

    pos_a, names, arrays_a = gathered(*first_hops(PAIRS[0]), ())
    even_b, odd_b = first_hops(PAIRS[1])
    pos_b, names, arrays_b = gathered(even_b, odd_b, tuple(arrays_a))
    arrays_a = [arrays_a[0], *ordered(tuple(arrays_a[1:]), (*even_b[1:], *odd_b[1:]))]
    carried = units(0, names, arrays_a, [], (arrays_b[0],))
    arrays_b = [arrays_b[0], *ordered(tuple(arrays_b[1:]), (carried[2],))]
    parts_a = sums(0, carried, tuple(arrays_b[1:]))
    carried = units(1, names, arrays_b, carried, (parts_a[0],))
    x_all, g_all, hidden, grad_pre_gate, grad_pre_up = carried
    done, even_a, odd_a = first_step(parts_a[0], along_c(parts_a[1], -1), (hidden,))
    other_b, *lefts = partials_of_core(
        1, len(PAIRS), order, 1, carried[3:], weights, ranges, True, done
    )
    done, even_a, odd_a = second_step(pos_a, even_a, odd_a, (other_b,))
    other_b = along_c(ordered(other_b, done), -1)
    (own_b,) = partials_of_core(1, len(PAIRS), order, 0, lefts, weights, ranges, False, done)
    done, even_b, odd_b = first_step(own_b, other_b, ())
    done_a, returned_a = third_step(PAIRS[0], pos_a, even_a, odd_a, done)
    grad_down = weight_grad(hidden, g_all, done + done_a)
    done, even_b, odd_b = second_step(pos_b, even_b, odd_b, (grad_down,))
    grad_gate = weight_grad(grad_pre_gate, x_all, done)
    done, returned_b = third_step(PAIRS[1], pos_b, even_b, odd_b, (grad_gate,))
    grad_up = weight_grad(grad_pre_up, x_all, done)
    grad_tokens = add_up(returned_a + returned_b)
    return (grad_tokens, grad_gate.T[None], grad_up.T[None], grad_down[None])


def solution(mesh):
    return jax.shard_map(
        local,
        mesh=mesh,
        in_specs=(
            P("ep", "etp"),
            P("ep", "etp"),
            P("ep", None),
            P("ep", None),
            P("ep", None, "etp"),
            P("ep", None, "etp"),
            P("ep", "etp", None),
        ),
        out_specs=(
            P("ep", "etp"),
            P("ep", None, "etp"),
            P("ep", None, "etp"),
            P("ep", "etp", None),
        ),
        check_vma=False,
    )
```

```python
import jax
import jax.numpy as jnp
from jax import lax
from jax.experimental import pallas as pl
from jax.experimental.pallas import tpu as pltpu
from jax.sharding import PartitionSpec as P

VMEM_LIMIT = 58 * 1024 * 1024
CORES = 2
DEPTH = 4
PAIRS = ((0, 1), (2, 3))
TILES = 6
ROUTING_ROWS = 16
ANY = pl.BlockSpec(memory_space=pl.ANY)
VMEM = pl.BlockSpec(memory_space=pltpu.VMEM)
SMEM = pl.BlockSpec(memory_space=pltpu.SMEM)


def product(left, right):
    return jnp.dot(left, right, preferred_element_type=jnp.float32)


def left_product(left, right):
    return lax.dot_general(
        left, right, (((0,), (0,)), ((), ())), preferred_element_type=jnp.float32
    )


def half(*shape):
    return jax.ShapeDtypeStruct(shape, jnp.bfloat16)


def right_product(left, right):
    return lax.dot_general(
        left, right, (((1,), (1,)), ((), ())), preferred_element_type=jnp.float32
    )


def full32(*shape):
    return jax.ShapeDtypeStruct(shape, jnp.float32)


def params():
    return pltpu.CompilerParams(vmem_limit_bytes=VMEM_LIMIT)


def shifted(value, axis, stride, count, step):
    step %= count
    if step == 0:
        return value
    pairs = []
    for src in range(lax.axis_size(axis)):
        place = src // stride % count
        pairs.append((src, src + ((place + step) % count - place) * stride))
    return lax.ppermute(value, axis, pairs)


def whole_call(kernel, args, out_shapes, experts=None, after=()):
    scalars = [] if experts is None else [experts]
    skipped = len(after)

    def body(*refs):
        kernel(*refs[skipped:])

    return pl.pallas_call(
        body,
        in_specs=[ANY] * skipped + [SMEM] * len(scalars) + [VMEM] * len(args),
        out_specs=[VMEM] * len(out_shapes),
        out_shape=out_shapes,
        compiler_params=params(),
        cost_estimate=pl.CostEstimate(flops=0, bytes_accessed=1, transcendentals=0),
    )(*after, *scalars, *args)


def pack(tokens, probs, expert_ids):
    tok_rows, width = tokens.shape

    def kernel(t_ref, p_ref, id_ref, out_ref):
        out_ref[:tok_rows, :] = t_ref[...]
        rest = p_ref[...]
        rows = [id_ref[...].astype(jnp.float32)]
        for _ in range(3):
            part = rest.astype(jnp.bfloat16).astype(jnp.float32)
            rows.append(part)
            rest = rest - part
        out_ref[tok_rows:, :] = jnp.zeros((ROUTING_ROWS, width), jnp.bfloat16)
        out_ref[tok_rows:, :tok_rows] = jnp.concatenate(rows, axis=0).astype(jnp.bfloat16)

    assert 4 * probs.shape[0] == ROUTING_ROWS
    return whole_call(
        kernel, [tokens, probs, expert_ids], [half(tok_rows + ROUTING_ROWS, width)]
    )[0]


def routes(ref, tok_rows, expert):
    rows = ref[tok_rows:, :tok_rows].astype(jnp.float32)
    top = ROUTING_ROWS // 4
    hit = rows[:top] == expert.astype(jnp.float32)
    weights = rows[top : 2 * top] + rows[2 * top : 3 * top] + rows[3 * top :]
    prob = jnp.sum(jnp.where(hit, weights, 0.0), axis=0, keepdims=True)
    named = jnp.sum(hit.astype(jnp.float32), axis=0, keepdims=True)
    before = lax.broadcasted_iota(jnp.int32, (tok_rows, tok_rows), 0)
    here = lax.broadcasted_iota(jnp.int32, (tok_rows, tok_rows), 1)
    ahead = (before < here).astype(jnp.float32).astype(jnp.bfloat16)
    many = jnp.broadcast_to(named, (8, tok_rows)).astype(jnp.bfloat16)
    pos = product(many, ahead)[:1]
    return jnp.where(named > 0.0, pos, -1.0).astype(jnp.int32), prob


def hits(pos, capacity):
    slots = lax.broadcasted_iota(jnp.int32, (capacity, pos.shape[1]), 0)
    return slots == pos


def one_hot(pos, capacity):
    return hits(pos, capacity).astype(jnp.float32).astype(jnp.bfloat16)


def pick_pair(experts, held_in, held_grad, capacity, after):
    steps, blocks, ranges = len(held_in), len(held_in[0]), len(held_grad[0])
    tok_rows, width = held_grad[0][0].shape
    rows = steps * blocks * capacity
    flat_in = [a for group in held_in for a in group]
    flat_grad = [a for group in held_grad for a in group]

    def kernel(e_ref, *refs):
        in_refs, refs = refs[: len(flat_in)], refs[len(flat_in) :]
        grad_refs, refs = refs[: len(flat_grad)], refs[len(flat_grad) :]
        keep_ref, in_out, grad_out, pos_ref = refs[0], refs[1], refs[2:-1], refs[-1]
        for i, ref in enumerate(in_refs):
            pos, _ = routes(ref, tok_rows, e_ref[0])
            chosen = hits(pos, capacity).astype(jnp.float32).astype(jnp.bfloat16)
            value = product(chosen, ref[:tok_rows, :]).astype(jnp.bfloat16)
            keep_ref[i * capacity : (i + 1) * capacity, :] = value
            in_out[i * capacity : (i + 1) * capacity, :] = value
        for k in range(steps):
            for dx in range(blocks):
                pos, prob = routes(in_refs[k * blocks], tok_rows, e_ref[dx])
                pos_ref[k, dx] = pos
                hit = hits(pos, capacity)
                chosen = hit.astype(jnp.float32).astype(jnp.bfloat16)
                weight = jnp.sum(jnp.where(hit, prob, 0.0), axis=1, keepdims=True)
                for dy in range(ranges):
                    start = (dy * steps + k) * capacity + (rows if dx == 0 else 0)
                    out_ref = keep_ref if dx == 0 else grad_out[dx - 1]
                    value = weight * product(chosen, grad_refs[k * ranges + dy][...])
                    out_ref[start : start + capacity, :] = value.astype(jnp.bfloat16)

    grad_rows = ranges * steps * capacity
    shapes = [half(rows + grad_rows, width), half(rows, width)]
    shapes += [half(grad_rows, width)] * (blocks - 1)
    shapes += [jax.ShapeDtypeStruct((steps, blocks, 1, tok_rows), jnp.int32)]
    outs = whole_call(kernel, [*flat_in, *flat_grad], shapes, experts, after)
    return outs[:-1], outs[-1]


def fixed(a):
    return pl.BlockSpec(a.shape, lambda f, *_: (0,) * a.ndim)


def hidden_units(chunk, chunks, order, names, pieces, weights, sizes, carried, after):
    ff, full = weights[0].shape
    blocks, ranges, capacity = sizes
    tile, width, k_rows = ff // TILES, pieces[0].shape[1], blocks * capacity
    rows, n_in = 2 * k_rows, len(pieces)

    def kernel(order_ref, *refs):
        in_refs, refs = refs[:n_in], refs[n_in:]
        (wg_ref, wu_ref, wd_ref), refs = refs[:3], refs[3 + len(carried) + len(after) :]
        x_ref, g_ref, hid_ref, gpg_ref, gpu_ref = refs

        def columns(dc, dy):
            at = order_ref[dc * ranges + dy] * width
            return pl.ds(pl.multiple_of(at, width), width)

        def put_grad(d, dc, ref, first):
            for dy in range(ranges):
                for k in range(2):
                    start = k * k_rows + d * capacity
                    at = first + (dy * 2 + k) * capacity
                    g_ref[start : start + capacity, columns(dc, dy)] = ref[at : at + capacity, :]

        @pl.when(pl.program_id(0) == 0)
        def _():
            for (kind, d, dc), ref in zip(names, in_refs):
                if kind == "grad":
                    put_grad(d, dc, ref, 0)
                else:
                    x_ref[:, columns(dc, d)] = ref[:rows, :]
                    if kind == "keep":
                        put_grad(0, dc, ref, rows)

        gate = right_product(x_ref[...], wg_ref[...])
        up = right_product(x_ref[...], wu_ref[...])
        sig = jax.nn.sigmoid(gate)
        silu = gate * sig
        hid_ref[...] = (silu * up).astype(jnp.bfloat16).T
        slope = up * sig * (1.0 + gate * (1.0 - sig))
        grad_hidden = right_product(g_ref[...], wd_ref[...])
        gpg_ref[...] = (grad_hidden * slope).astype(jnp.bfloat16).T
        gpu_ref[...] = (grad_hidden * silu).astype(jnp.bfloat16).T

    out_shapes = [half(chunks * rows, full)] * 2 + [half(ff, chunks * rows)] * 3
    out_specs = [pl.BlockSpec((rows, full), lambda f, _: (chunk, 0))] * 2
    out_specs += [pl.BlockSpec((tile, rows), lambda f, _: (f, chunk))] * 3
    in_specs = [fixed(a) for a in pieces]
    in_specs += [pl.BlockSpec((tile, full), lambda f, _: (f, 0))] * 3
    first = 1 + len(in_specs)
    in_specs += [ANY] * (len(carried) + len(after))
    return pl.pallas_call(
        kernel,
        grid_spec=pltpu.PrefetchScalarGridSpec(
            num_scalar_prefetch=1, grid=(TILES,), in_specs=in_specs, out_specs=out_specs
        ),
        out_shape=out_shapes,
        input_output_aliases={first + i: i for i in range(len(carried))},
        compiler_params=params(),
        cost_estimate=pl.CostEstimate(
            flops=6 * rows * ff * full,
            bytes_accessed=6 * ff * full + 8 * rows * full + 6 * rows * ff,
            transcendentals=rows * ff,
        ),
    )(order, *pieces, *weights, *carried, *after)


def partials(chunk, chunks, order, lefts, weights, ranges, after):
    ff, full = weights[0].shape
    rows = lefts[0].shape[1] // chunks
    steps = CORES * ranges
    width = full // steps

    def kernel(order_ref, gpg_ref, gpu_ref, wg_ref, wu_ref, *refs):
        own_ref, other_ref, lg_ref, lu_ref = refs[len(after) :]
        step = pl.program_id(0)

        @pl.when(step == 0)
        def _():
            lg_ref[...] = gpg_ref[...].T
            lu_ref[...] = gpu_ref[...].T

        value = product(lg_ref[...], wg_ref[...]) + product(lu_ref[...], wu_ref[...])

        @pl.when(step < ranges)
        def _():
            other_ref[0] = value.astype(jnp.bfloat16)

        @pl.when(step >= ranges)
        def _():
            own_ref[0] = value.astype(jnp.bfloat16)

    left = pl.BlockSpec((ff, rows), lambda r, _: (0, chunk))
    right = pl.BlockSpec((ff, width), lambda r, order: (0, order[lax.rem(r + ranges, steps)]))
    own = pl.BlockSpec((1, rows, width), lambda r, _: (jnp.maximum(r - ranges, 0), 0, 0))
    other = pl.BlockSpec((1, rows, width), lambda r, _: (jnp.minimum(r, ranges - 1), 0, 0))
    return pl.pallas_call(
        kernel,
        grid_spec=pltpu.PrefetchScalarGridSpec(
            num_scalar_prefetch=1,
            grid=(steps,),
            in_specs=[left, left, right, right] + [ANY] * len(after),
            out_specs=[own, other],
            scratch_shapes=[pltpu.VMEM((rows, ff), jnp.bfloat16)] * 2,
        ),
        out_shape=[half(ranges, rows, width)] * 2,
        compiler_params=params(),
        cost_estimate=pl.CostEstimate(
            flops=4 * rows * ff * full,
            bytes_accessed=4 * ff * full + 2 * rows * full + 4 * rows * ff,
            transcendentals=0,
        ),
    )(order, *lefts, *weights[:2], *after)


def partials_of_core(chunk, chunks, order, dc, lefts, weights, ranges, turn, after):
    ff, full = weights[0].shape
    rows = lefts[0].shape[1] // chunks if turn else lefts[0].shape[0]
    width = full // (CORES * ranges)

    def kernel(order_ref, lg_ref, lu_ref, wg_ref, wu_ref, *refs):
        refs = refs[len(after) :]
        if turn:

            @pl.when(pl.program_id(0) == 0)
            def _():
                refs[1][...] = lg_ref[...].T
                refs[2][...] = lu_ref[...].T

            lg_ref, lu_ref = refs[1:]
        value = product(lg_ref[...], wg_ref[...]) + product(lu_ref[...], wu_ref[...])
        refs[0][0] = value.astype(jnp.bfloat16)

    right = pl.BlockSpec((ff, width), lambda r, order: (0, order[dc * ranges + r]))
    turned = pl.BlockSpec((rows, ff), lambda r, _: (0, 0))
    left = pl.BlockSpec((ff, rows), lambda r, _: (0, chunk)) if turn else turned
    return pl.pallas_call(
        kernel,
        grid_spec=pltpu.PrefetchScalarGridSpec(
            num_scalar_prefetch=1,
            grid=(ranges,),
            in_specs=[left, left, right, right] + [ANY] * len(after),
            out_specs=[pl.BlockSpec((1, rows, width), lambda r, _: (r, 0, 0))]
            + [turned] * (2 * turn),
        ),
        out_shape=[half(ranges, rows, width)] + [half(rows, ff)] * (2 * turn),
        compiler_params=params(),
        cost_estimate=pl.CostEstimate(
            flops=4 * rows * ff * full // CORES,
            bytes_accessed=2 * ff * full + rows * full + 4 * rows * ff,
            transcendentals=0,
        ),
    )(order, *lefts, *weights[:2], *after)


def weight_grad(left, right, after):
    return product(ordered(left, after), right).astype(jnp.bfloat16)


def first_returns(own, other, sizes):
    blocks, ranges, capacity = sizes

    def total(at):
        value = own[at].astype(jnp.float32) + other[at].astype(jnp.float32)
        return value.astype(jnp.bfloat16)

    k_rows = blocks * capacity
    even = [total((dy, slice(0, k_rows))) for dy in range(ranges)]
    starts = [k_rows + dx * capacity for dx in range(blocks)]
    return even, [total((slice(None), slice(at, at + capacity))) for at in starts]


def spread(pos, rows):
    chosen = hits(pos, rows.shape[0]).astype(jnp.float32).astype(jnp.bfloat16)
    return left_product(chosen, rows)


def second_returns(pos, even, odd, after):
    ranges, blocks = len(even), len(odd)
    tok_rows, width = pos.shape[3], even[0].shape[1]
    capacity = even[0].shape[0] // blocks

    def kernel(pos_ref, *refs):
        even_refs, refs = refs[:ranges], refs[ranges:]
        odd_refs, out_refs = refs[:blocks], refs[blocks:]
        for dx in range(blocks):
            rows = slice(dx * capacity, (dx + 1) * capacity)
            value = even_refs[0][rows, :].astype(jnp.float32)
            for dy in range(1, ranges):
                value += even_refs[dy][rows, :].astype(jnp.float32)
            out_refs[dx][...] = value.astype(jnp.bfloat16)
        for dy in range(ranges):
            value = spread(pos_ref[1, 0], odd_refs[0][dy])
            for dx in range(1, blocks):
                value += spread(pos_ref[1, dx], odd_refs[dx][dy])
            out_refs[blocks + dy][...] = value.astype(jnp.bfloat16)

    shapes = [half(capacity, width)] * blocks + [half(tok_rows, width)] * ranges
    outs = whole_call(kernel, [pos, *even, *odd], shapes, after=after)
    return outs[:blocks], outs[blocks:]


def third_returns(pos, even, odd, after):
    blocks, ranges = len(even), len(odd)
    tok_rows, width = pos.shape[3], even[0].shape[1]

    def kernel(pos_ref, *refs):
        even_refs, refs = refs[:blocks], refs[blocks:]
        odd_refs, out_refs = refs[:ranges], refs[ranges:]
        value = spread(pos_ref[0, 0], even_refs[0][...])
        for dx in range(1, blocks):
            value += spread(pos_ref[0, dx], even_refs[dx][...])
        out_refs[0][...] = value.astype(jnp.bfloat16)
        value = odd_refs[0][...].astype(jnp.float32)
        for dy in range(1, ranges):
            value += odd_refs[dy][...].astype(jnp.float32)
        out_refs[1][...] = value.astype(jnp.bfloat16)

    return whole_call(kernel, [pos, *even, *odd], [half(tok_rows, width)] * 2, after=after)


def add_up(parts):
    value = parts[0].astype(jnp.float32)
    for part in parts[1:]:
        value += part.astype(jnp.float32)
    return value.astype(jnp.bfloat16)


def ordered(value, after):
    return lax.optimization_barrier((value, tuple(after)))[0] if after else value


def local(tokens, grad_out, probs, expert_ids, w_gate, w_up, w_down):
    experts, etp = lax.axis_size("ep"), lax.axis_size("etp")
    blocks, ranges = experts // DEPTH, etp // CORES
    tok_rows, top_count = expert_ids.shape
    capacity = 3 * tok_rows * top_count // (2 * experts)
    me, mine = lax.axis_index("ep"), lax.axis_index("etp")
    my_z, my_x = me // blocks, me % blocks
    my_y, my_c = mine // CORES, mine % CORES

    def along_z(value, step):
        return shifted(value, "ep", blocks, DEPTH, step)

    def along_x(value, step):
        return shifted(value, "ep", 1, blocks, step)

    def along_y(value, step):
        return shifted(value, "etp", CORES, ranges, step)

    def along_c(value, step):
        return shifted(value, "etp", 1, CORES, step)

    own_experts = jnp.stack([my_z * blocks + (my_x + dx) % blocks for dx in range(blocks)])
    own_experts = own_experts.astype(jnp.int32)
    order = [
        (my_y - dy) % ranges * CORES + (my_c - dc) % CORES
        for dc in range(CORES)
        for dy in range(ranges)
    ]
    order = jnp.stack(order).astype(jnp.int32)
    weights = (w_gate[0].T, w_up[0].T, w_down[0])

    def first_hops(line):
        even = [[along_x(line[k], dx) for dx in range(blocks)] for k in EVEN]
        odd = [[along_y(line[k], dy) for dy in range(ranges)] for k in ODD]
        return list(zip(even, odd))

    def second_hops(outs):
        keep, even, odd = outs[0], outs[1], outs[2:]
        names, arrays = [("keep", 0)], [keep]
        for dy in range(1, ranges):
            names.append(("even", dy))
            arrays.append(along_y(even, dy))
        for dx in range(1, blocks):
            names.append(("odd", dx))
            arrays.append(along_x(odd[dx - 1], dx))
        return names, arrays

    def core_hops(hopped):
        names, arrays = [], []
        for pair, (kinds, values) in enumerate(hopped):
            for (kind, d), value in zip(kinds, values):
                for dc in range(CORES):
                    names.append((pair, kind, d, dc))
                    arrays.append(along_c(value, dc))
        return names, arrays

    sizes = (blocks, ranges, capacity)
    packed = pack(tokens, probs.T, expert_ids.T)

    def z_line(value):
        near = along_z(value, 1)
        return [value, near, along_z(near, 1), along_z(value, 3)]

    in_line, grad_line = z_line(packed), z_line(grad_out)

    def first_hops(pair):
        held_in = [[along_x(in_line[k], dx) for dx in range(blocks)] for k in pair]
        return held_in, [[along_y(grad_line[k], dy) for dy in range(ranges)] for k in pair]

    def gathered(held_in, held_grad, after):
        outs, pos = pick_pair(own_experts, held_in, held_grad, capacity, after)
        names, arrays = [("keep", 0)], [outs[0]]
        for dy in range(1, ranges):
            names.append(("in", dy))
            arrays.append(along_y(outs[1], dy))
        for dx in range(1, blocks):
            names.append(("grad", dx))
            arrays.append(along_x(outs[1 + dx], dx))
        return pos, names, arrays

    def units(chunk, names, arrays, carried, after):
        names = [(kind, d, dc) for kind, d in names for dc in range(CORES)]
        pieces = [along_c(a, dc) for a in arrays for dc in range(CORES)]
        return hidden_units(
            chunk, len(PAIRS), order, names, pieces, weights, sizes, carried, after
        )

    def sums(chunk, carried, after):
        return partials(chunk, len(PAIRS), order, carried[3:], weights, ranges, after)

    def first_step(own, other, after):
        even, odd = first_returns(*ordered((own, other), after), sizes)
        arrived = [along_y(a, -dy) for dy, a in enumerate(even)]
        return (*even, *odd), arrived, [along_x(a, -dx) for dx, a in enumerate(odd)]

    def second_step(pos, even, odd, after):
        even, odd = second_returns(pos, even, odd, after)
        arrived = [along_x(a, -dx) for dx, a in enumerate(even)]
        return (*even, *odd), arrived, [along_y(a, -dy) for dy, a in enumerate(odd)]

    def third_step(pair, pos, even, odd, after):
        outs = third_returns(pos, even, odd, after)
        return tuple(outs), [along_z(a, -k) for k, a in zip(pair, outs)]

    pos_a, names, arrays_a = gathered(*first_hops(PAIRS[0]), ())
    held_b = first_hops(PAIRS[1])
    pos_b, names, arrays_b = gathered(*held_b, tuple(arrays_a))
    before = tuple(a for held in held_b for group in held for a in group[1:])
    arrays_a = [arrays_a[0], *ordered(tuple(arrays_a[1:]), before)]
    carried = units(0, names, arrays_a, [], (arrays_b[0],))
    arrays_b = [arrays_b[0], *ordered(tuple(arrays_b[1:]), (carried[2],))]
    parts_a = sums(0, carried, tuple(arrays_b[1:]))
    carried = units(1, names, arrays_b, carried, (parts_a[0],))
    x_all, g_all, hidden, grad_pre_gate, grad_pre_up = carried
    done, even_a, odd_a = first_step(parts_a[0], along_c(parts_a[1], -1), (hidden,))
    other_b, *lefts = partials_of_core(
        1, len(PAIRS), order, 1, carried[3:], weights, ranges, True, done
    )
    done, even_a, odd_a = second_step(pos_a, even_a, odd_a, (other_b,))
    other_b = along_c(ordered(other_b, done), -1)
    (own_b,) = partials_of_core(1, len(PAIRS), order, 0, lefts, weights, ranges, False, done)
    done, even_b, odd_b = first_step(own_b, other_b, ())
    done_a, returned_a = third_step(PAIRS[0], pos_a, even_a, odd_a, done)
    grad_down = weight_grad(hidden, g_all, done + done_a)
    done, even_b, odd_b = second_step(pos_b, even_b, odd_b, (grad_down,))
    grad_gate = weight_grad(grad_pre_gate, x_all, done)
    done, returned_b = third_step(PAIRS[1], pos_b, even_b, odd_b, (grad_gate,))
    grad_up = weight_grad(grad_pre_up, x_all, done)
    grad_tokens = add_up(returned_a + returned_b)
    return (grad_tokens, grad_gate.T[None], grad_up.T[None], grad_down[None])


def solution(mesh):
    return jax.shard_map(
        local,
        mesh=mesh,
        in_specs=(
            P("ep", "etp"),
            P("ep", "etp"),
            P("ep", None),
            P("ep", None),
            P("ep", None, "etp"),
            P("ep", None, "etp"),
            P("ep", "etp", None),
        ),
        out_specs=(
            P("ep", "etp"),
            P("ep", None, "etp"),
            P("ep", None, "etp"),
            P("ep", "etp", None),
        ),
        check_vma=False,
    )
```

```python
import jax
import jax.numpy as jnp
from jax import lax
from jax.experimental import pallas as pl
from jax.experimental.pallas import tpu as pltpu
from jax.sharding import PartitionSpec as P

VMEM_LIMIT = 58 * 1024 * 1024
CORES = 2
DEPTH = 4
PAIRS = ((0, 1), (2, 3))
TILES = 6
ROUTING_ROWS = 16
ANY = pl.BlockSpec(memory_space=pl.ANY)
VMEM = pl.BlockSpec(memory_space=pltpu.VMEM)
SMEM = pl.BlockSpec(memory_space=pltpu.SMEM)


def product(left, right):
    return jnp.dot(left, right, preferred_element_type=jnp.float32)


def left_product(left, right):
    return lax.dot_general(
        left, right, (((0,), (0,)), ((), ())), preferred_element_type=jnp.float32
    )


def half(*shape):
    return jax.ShapeDtypeStruct(shape, jnp.bfloat16)


def right_product(left, right):
    return lax.dot_general(
        left, right, (((1,), (1,)), ((), ())), preferred_element_type=jnp.float32
    )


def full32(*shape):
    return jax.ShapeDtypeStruct(shape, jnp.float32)


def params():
    return pltpu.CompilerParams(vmem_limit_bytes=VMEM_LIMIT)


def shifted(value, axis, stride, count, step):
    step %= count
    if step == 0:
        return value
    pairs = []
    for src in range(lax.axis_size(axis)):
        place = src // stride % count
        pairs.append((src, src + ((place + step) % count - place) * stride))
    return lax.ppermute(value, axis, pairs)


def whole_call(kernel, args, out_shapes, experts=None, after=()):
    scalars = [] if experts is None else [experts]
    skipped = len(after)

    def body(*refs):
        kernel(*refs[skipped:])

    return pl.pallas_call(
        body,
        in_specs=[ANY] * skipped + [SMEM] * len(scalars) + [VMEM] * len(args),
        out_specs=[VMEM] * len(out_shapes),
        out_shape=out_shapes,
        compiler_params=params(),
        cost_estimate=pl.CostEstimate(flops=0, bytes_accessed=1, transcendentals=0),
    )(*after, *scalars, *args)


def pack(tokens, grad_out, probs, expert_ids):
    tok_rows, width = tokens.shape

    def kernel(t_ref, g_ref, p_ref, id_ref, out_ref):
        out_ref[:tok_rows, :] = t_ref[...]
        out_ref[tok_rows : 2 * tok_rows, :] = g_ref[...]
        rest = p_ref[...]
        rows = [id_ref[...].astype(jnp.float32)]
        for _ in range(3):
            part = rest.astype(jnp.bfloat16).astype(jnp.float32)
            rows.append(part)
            rest = rest - part
        out_ref[2 * tok_rows :, :] = jnp.zeros((ROUTING_ROWS, width), jnp.bfloat16)
        out_ref[2 * tok_rows :, :tok_rows] = jnp.concatenate(rows, axis=0).astype(jnp.bfloat16)

    assert 4 * probs.shape[0] == ROUTING_ROWS
    return whole_call(
        kernel, [tokens, grad_out, probs, expert_ids], [half(2 * tok_rows + ROUTING_ROWS, width)]
    )[0]


def routes(ref, tok_rows, expert):
    rows = ref[2 * tok_rows :, :tok_rows].astype(jnp.float32)
    top = ROUTING_ROWS // 4
    hit = rows[:top] == expert.astype(jnp.float32)
    weights = rows[top : 2 * top] + rows[2 * top : 3 * top] + rows[3 * top :]
    prob = jnp.sum(jnp.where(hit, weights, 0.0), axis=0, keepdims=True)
    named = jnp.sum(hit.astype(jnp.float32), axis=0, keepdims=True)
    before = lax.broadcasted_iota(jnp.int32, (tok_rows, tok_rows), 0)
    here = lax.broadcasted_iota(jnp.int32, (tok_rows, tok_rows), 1)
    ahead = (before < here).astype(jnp.float32).astype(jnp.bfloat16)
    many = jnp.broadcast_to(named, (8, tok_rows)).astype(jnp.bfloat16)
    pos = product(many, ahead)[:1]
    return jnp.where(named > 0.0, pos, -1.0).astype(jnp.int32), prob


def hits(pos, capacity):
    slots = lax.broadcasted_iota(jnp.int32, (capacity, pos.shape[1]), 0)
    return slots == pos


def one_hot(pos, capacity):
    return hits(pos, capacity).astype(jnp.float32).astype(jnp.bfloat16)


def pick_pair(experts, even, odd, capacity, after):
    blocks, ranges = len(even), len(odd)
    tok_rows, width = (even[0].shape[0] - ROUTING_ROWS) // 2, even[0].shape[1]

    def kernel(e_ref, *refs):
        even_refs, refs = refs[:blocks], refs[blocks:]
        odd_refs, refs = refs[:ranges], refs[ranges:]
        keep_ref, even_out, odd_out, pos_ref = refs[0], refs[1], refs[2:-1], refs[-1]

        def picked(ref, pos, prob):
            hit = hits(pos, capacity)
            chosen = hit.astype(jnp.float32).astype(jnp.bfloat16)
            weight = jnp.sum(jnp.where(hit, prob, 0.0), axis=1, keepdims=True)
            rows = product(chosen, ref[:tok_rows, :])
            grads = product(chosen, ref[tok_rows : 2 * tok_rows, :])
            return rows.astype(jnp.bfloat16), (weight * grads).astype(jnp.bfloat16)

        for dx in range(blocks):
            pos, prob = routes(even_refs[dx], tok_rows, e_ref[0])
            rows = slice(dx * capacity, (dx + 1) * capacity)
            for i, value in enumerate(picked(even_refs[dx], pos, prob)):
                keep_ref[i, rows, :] = value
                even_out[i, rows, :] = value
            pos_ref[1, dx] = routes(even_refs[0], tok_rows, e_ref[dx])[0]
        for dx in range(blocks):
            pos, prob = routes(odd_refs[0], tok_rows, e_ref[dx])
            pos_ref[0, dx] = pos
            for dy in range(ranges):
                start = (blocks + dy if dx == 0 else dy) * capacity
                out_ref = keep_ref if dx == 0 else odd_out[dx - 1]
                for i, value in enumerate(picked(odd_refs[dy], pos, prob)):
                    out_ref[i, start : start + capacity, :] = value

    shapes = [half(2, (blocks + ranges) * capacity, width), half(2, blocks * capacity, width)]
    shapes += [half(2, ranges * capacity, width)] * (blocks - 1)
    shapes += [jax.ShapeDtypeStruct((2, blocks, 1, tok_rows), jnp.int32)]
    outs = whole_call(kernel, [*even, *odd], shapes, experts, after)
    return outs[:-1], outs[-1]


def fixed(a):
    return pl.BlockSpec(a.shape, lambda f, *_: (0,) * a.ndim)


def hidden_units(chunk, chunks, order, names, pieces, weights, sizes, carried, after):
    ff, full = weights[0].shape
    blocks, ranges, capacity = sizes
    tile, width, k_rows = ff // TILES, pieces[0].shape[2], blocks * capacity
    rows, n_in = 2 * k_rows, len(pieces)

    def kernel(order_ref, *refs):
        in_refs, refs = refs[:n_in], refs[n_in:]
        (wg_ref, wu_ref, wd_ref), refs = refs[:3], refs[3 + len(carried) + len(after) :]
        x_ref, g_ref, hid_ref, gpg_ref, gpu_ref = refs

        def columns(dc, dy):
            at = order_ref[dc * ranges + dy] * width
            return pl.ds(pl.multiple_of(at, width), width)

        def put(out_ref, i):
            for (kind, d, dc), ref in zip(names, in_refs):
                if kind == "even":
                    out_ref[:k_rows, columns(dc, d)] = ref[i]
                    continue
                start = k_rows + d * capacity
                first = k_rows if kind == "keep" else 0
                if kind == "keep":
                    out_ref[:k_rows, columns(dc, 0)] = ref[i, :k_rows, :]
                for dy in range(ranges):
                    at = first + dy * capacity
                    out_ref[start : start + capacity, columns(dc, dy)] = ref[
                        i, at : at + capacity, :
                    ]

        @pl.when(pl.program_id(0) == 0)
        def _():
            put(x_ref, 0)
            put(g_ref, 1)

        gate = right_product(x_ref[...], wg_ref[...])
        up = right_product(x_ref[...], wu_ref[...])
        sig = jax.nn.sigmoid(gate)
        silu = gate * sig
        hid_ref[...] = (silu * up).astype(jnp.bfloat16).T
        slope = up * sig * (1.0 + gate * (1.0 - sig))
        grad_hidden = right_product(g_ref[...], wd_ref[...])
        gpg_ref[...] = (grad_hidden * slope).astype(jnp.bfloat16).T
        gpu_ref[...] = (grad_hidden * silu).astype(jnp.bfloat16).T

    out_shapes = [half(chunks * rows, full)] * 2 + [half(ff, chunks * rows)] * 3
    out_specs = [pl.BlockSpec((rows, full), lambda f, _: (chunk, 0))] * 2
    out_specs += [pl.BlockSpec((tile, rows), lambda f, _: (f, chunk))] * 3
    in_specs = [fixed(a) for a in pieces]
    in_specs += [pl.BlockSpec((tile, full), lambda f, _: (f, 0))] * 3
    first = 1 + len(in_specs)
    in_specs += [ANY] * (len(carried) + len(after))
    return pl.pallas_call(
        kernel,
        grid_spec=pltpu.PrefetchScalarGridSpec(
            num_scalar_prefetch=1, grid=(TILES,), in_specs=in_specs, out_specs=out_specs
        ),
        out_shape=out_shapes,
        input_output_aliases={first + i: i for i in range(len(carried))},
        compiler_params=params(),
        cost_estimate=pl.CostEstimate(
            flops=6 * rows * ff * full,
            bytes_accessed=6 * ff * full + 8 * rows * full + 6 * rows * ff,
            transcendentals=rows * ff,
        ),
    )(order, *pieces, *weights, *carried, *after)


def partials(chunk, chunks, order, lefts, weights, ranges, after):
    ff, full = weights[0].shape
    rows = lefts[0].shape[1] // chunks
    steps = CORES * ranges
    width = full // steps

    def kernel(order_ref, gpg_ref, gpu_ref, wg_ref, wu_ref, *refs):
        own_ref, other_ref, lg_ref, lu_ref = refs[len(after) :]
        step = pl.program_id(0)

        @pl.when(step == 0)
        def _():
            lg_ref[...] = gpg_ref[...].T
            lu_ref[...] = gpu_ref[...].T

        value = product(lg_ref[...], wg_ref[...]) + product(lu_ref[...], wu_ref[...])

        @pl.when(step < ranges)
        def _():
            other_ref[0] = value.astype(jnp.bfloat16)

        @pl.when(step >= ranges)
        def _():
            own_ref[0] = value.astype(jnp.bfloat16)

    left = pl.BlockSpec((ff, rows), lambda r, _: (0, chunk))
    right = pl.BlockSpec((ff, width), lambda r, order: (0, order[lax.rem(r + ranges, steps)]))
    own = pl.BlockSpec((1, rows, width), lambda r, _: (jnp.maximum(r - ranges, 0), 0, 0))
    other = pl.BlockSpec((1, rows, width), lambda r, _: (jnp.minimum(r, ranges - 1), 0, 0))
    return pl.pallas_call(
        kernel,
        grid_spec=pltpu.PrefetchScalarGridSpec(
            num_scalar_prefetch=1,
            grid=(steps,),
            in_specs=[left, left, right, right] + [ANY] * len(after),
            out_specs=[own, other],
            scratch_shapes=[pltpu.VMEM((rows, ff), jnp.bfloat16)] * 2,
        ),
        out_shape=[half(ranges, rows, width)] * 2,
        compiler_params=params(),
        cost_estimate=pl.CostEstimate(
            flops=4 * rows * ff * full,
            bytes_accessed=4 * ff * full + 2 * rows * full + 4 * rows * ff,
            transcendentals=0,
        ),
    )(order, *lefts, *weights[:2], *after)


def partials_of_core(chunk, chunks, order, dc, lefts, weights, ranges, turn, after):
    ff, full = weights[0].shape
    rows = lefts[0].shape[1] // chunks if turn else lefts[0].shape[0]
    width = full // (CORES * ranges)

    def kernel(order_ref, lg_ref, lu_ref, wg_ref, wu_ref, *refs):
        refs = refs[len(after) :]
        if turn:

            @pl.when(pl.program_id(0) == 0)
            def _():
                refs[1][...] = lg_ref[...].T
                refs[2][...] = lu_ref[...].T

            lg_ref, lu_ref = refs[1:]
        value = product(lg_ref[...], wg_ref[...]) + product(lu_ref[...], wu_ref[...])
        refs[0][0] = value.astype(jnp.bfloat16)

    right = pl.BlockSpec((ff, width), lambda r, order: (0, order[dc * ranges + r]))
    turned = pl.BlockSpec((rows, ff), lambda r, _: (0, 0))
    left = pl.BlockSpec((ff, rows), lambda r, _: (0, chunk)) if turn else turned
    return pl.pallas_call(
        kernel,
        grid_spec=pltpu.PrefetchScalarGridSpec(
            num_scalar_prefetch=1,
            grid=(ranges,),
            in_specs=[left, left, right, right] + [ANY] * len(after),
            out_specs=[pl.BlockSpec((1, rows, width), lambda r, _: (r, 0, 0))]
            + [turned] * (2 * turn),
        ),
        out_shape=[half(ranges, rows, width)] + [half(rows, ff)] * (2 * turn),
        compiler_params=params(),
        cost_estimate=pl.CostEstimate(
            flops=4 * rows * ff * full // CORES,
            bytes_accessed=2 * ff * full + rows * full + 4 * rows * ff,
            transcendentals=0,
        ),
    )(order, *lefts, *weights[:2], *after)


def weight_grad(left, right, after):
    return product(ordered(left, after), right).astype(jnp.bfloat16)


def first_returns(own, other, sizes):
    blocks, ranges, capacity = sizes

    def total(at):
        value = own[at].astype(jnp.float32) + other[at].astype(jnp.float32)
        return value.astype(jnp.bfloat16)

    k_rows = blocks * capacity
    even = [total((dy, slice(0, k_rows))) for dy in range(ranges)]
    starts = [k_rows + dx * capacity for dx in range(blocks)]
    return even, [total((slice(None), slice(at, at + capacity))) for at in starts]


def spread(pos, rows):
    chosen = hits(pos, rows.shape[0]).astype(jnp.float32).astype(jnp.bfloat16)
    return left_product(chosen, rows)


def second_sums(pos_ref, even_refs, odd_refs, out_refs):
    ranges, blocks = len(even_refs), len(odd_refs)
    capacity = even_refs[0].shape[0] // blocks
    for dx in range(blocks):
        rows = slice(dx * capacity, (dx + 1) * capacity)
        value = even_refs[0][rows, :].astype(jnp.float32)
        for dy in range(1, ranges):
            value += even_refs[dy][rows, :].astype(jnp.float32)
        out_refs[dx][...] = value.astype(jnp.bfloat16)
    for dy in range(ranges):
        value = spread(pos_ref[0, 0], odd_refs[0][dy])
        for dx in range(1, blocks):
            value += spread(pos_ref[0, dx], odd_refs[dx][dy])
        out_refs[blocks + dy][...] = value.astype(jnp.bfloat16)


def third_sums(pos_ref, even_refs, odd_refs, out_refs):
    value = spread(pos_ref[1, 0], even_refs[0][...])
    for dx in range(1, len(even_refs)):
        value += spread(pos_ref[1, dx], even_refs[dx][...])
    out_refs[0][...] = value.astype(jnp.bfloat16)
    value = odd_refs[0][...].astype(jnp.float32)
    for ref in odd_refs[1:]:
        value += ref[...].astype(jnp.float32)
    out_refs[1][...] = value.astype(jnp.bfloat16)


def return_sums(second, third, after):
    args, shapes, works = [], [], []
    for body, held in ((second_sums, second), (third_sums, third)):
        if held is None:
            continue
        pos, even, odd = held
        tok_rows, width = pos.shape[3], even[0].shape[1]
        outs = [half(tok_rows, width)] * 2
        if body is second_sums:
            outs = [half(even[0].shape[0] // len(odd), width)] * len(odd)
            outs += [half(tok_rows, width)] * len(even)
        works.append((body, len(args), len(even), len(odd), len(shapes), len(outs)))
        args += [pos, *even, *odd]
        shapes += outs

    def kernel(*refs):
        in_refs, out_refs = refs[: len(args)], refs[len(args) :]
        for body, at, evens, odds, out_at, count in works:
            even_at = at + 1
            odd_at = even_at + evens
            body(
                in_refs[at],
                in_refs[even_at:odd_at],
                in_refs[odd_at : odd_at + odds],
                out_refs[out_at : out_at + count],
            )

    outs = whole_call(kernel, args, shapes, after=after)
    return [outs[out_at : out_at + count] for *_, out_at, count in works]


def add_up(parts):
    value = parts[0].astype(jnp.float32)
    for part in parts[1:]:
        value += part.astype(jnp.float32)
    return value.astype(jnp.bfloat16)


def ordered(value, after):
    return lax.optimization_barrier((value, tuple(after)))[0] if after else value


def local(tokens, grad_out, probs, expert_ids, w_gate, w_up, w_down):
    experts, etp = lax.axis_size("ep"), lax.axis_size("etp")
    blocks, ranges = experts // DEPTH, etp // CORES
    tok_rows, top_count = expert_ids.shape
    capacity = 3 * tok_rows * top_count // (2 * experts)
    me, mine = lax.axis_index("ep"), lax.axis_index("etp")
    my_z, my_x = me // blocks, me % blocks
    my_y, my_c = mine // CORES, mine % CORES

    def along_z(value, step):
        return shifted(value, "ep", blocks, DEPTH, step)

    def along_x(value, step):
        return shifted(value, "ep", 1, blocks, step)

    def along_y(value, step):
        return shifted(value, "etp", CORES, ranges, step)

    def along_c(value, step):
        return shifted(value, "etp", 1, CORES, step)

    own_experts = jnp.stack([my_z * blocks + (my_x + dx) % blocks for dx in range(blocks)])
    own_experts = own_experts.astype(jnp.int32)
    order = [
        (my_y - dy) % ranges * CORES + (my_c - dc) % CORES
        for dc in range(CORES)
        for dy in range(ranges)
    ]
    order = jnp.stack(order).astype(jnp.int32)
    weights = (w_gate[0].T, w_up[0].T, w_down[0])

    def first_hops(line):
        even = [[along_x(line[k], dx) for dx in range(blocks)] for k in EVEN]
        odd = [[along_y(line[k], dy) for dy in range(ranges)] for k in ODD]
        return list(zip(even, odd))

    def second_hops(outs):
        keep, even, odd = outs[0], outs[1], outs[2:]
        names, arrays = [("keep", 0)], [keep]
        for dy in range(1, ranges):
            names.append(("even", dy))
            arrays.append(along_y(even, dy))
        for dx in range(1, blocks):
            names.append(("odd", dx))
            arrays.append(along_x(odd[dx - 1], dx))
        return names, arrays

    def core_hops(hopped):
        names, arrays = [], []
        for pair, (kinds, values) in enumerate(hopped):
            for (kind, d), value in zip(kinds, values):
                for dc in range(CORES):
                    names.append((pair, kind, d, dc))
                    arrays.append(along_c(value, dc))
        return names, arrays

    sizes = (blocks, ranges, capacity)
    packed = pack(tokens, grad_out, probs.T, expert_ids.T)
    near = along_z(packed, 1)
    line = [packed, near, along_z(near, 1), along_z(packed, DEPTH - 1)]

    def first_hops(pair):
        even = [along_x(line[pair[0]], dx) for dx in range(blocks)]
        return even, [along_y(line[pair[1]], dy) for dy in range(ranges)]

    def gathered(even, odd, after):
        outs, pos = pick_pair(own_experts, even, odd, capacity, after)
        names, arrays = [("keep", 0)], [outs[0]]
        for dy in range(1, ranges):
            names.append(("even", dy))
            arrays.append(along_y(outs[1], dy))
        for dx in range(1, blocks):
            names.append(("odd", dx))
            arrays.append(along_x(outs[1 + dx], dx))
        return pos, names, arrays

    def units(chunk, names, arrays, carried, after):
        names = [(kind, d, dc) for kind, d in names for dc in range(CORES)]
        pieces = [along_c(a, dc) for a in arrays for dc in range(CORES)]
        return hidden_units(
            chunk, len(PAIRS), order, names, pieces, weights, sizes, carried, after
        )

    def sums(chunk, carried, after):
        return partials(chunk, len(PAIRS), order, carried[3:], weights, ranges, after)

    def first_step(own, other, after):
        even, odd = first_returns(*ordered((own, other), after), sizes)
        arrived = [along_y(a, -dy) for dy, a in enumerate(even)]
        return (*even, *odd), arrived, [along_x(a, -dx) for dx, a in enumerate(odd)]

    def second_hops(outs):
        arrived = [along_x(a, -dx) for dx, a in enumerate(outs[:blocks])]
        return arrived, [along_y(a, -dy) for dy, a in enumerate(outs[blocks:])]

    def third_hops(pair, outs):
        return [along_z(a, -k) for k, a in zip(pair, outs)]

    pos_a, names, arrays_a = gathered(*first_hops(PAIRS[0]), ())
    even_b, odd_b = first_hops(PAIRS[1])
    pos_b, names, arrays_b = gathered(even_b, odd_b, tuple(arrays_a))
    arrays_a = [arrays_a[0], *ordered(tuple(arrays_a[1:]), (*even_b[1:], *odd_b[1:]))]
    carried = units(0, names, arrays_a, [], (arrays_b[0],))
    arrays_b = [arrays_b[0], *ordered(tuple(arrays_b[1:]), (carried[2],))]
    parts_a = sums(0, carried, tuple(arrays_b[1:]))
    carried = units(1, names, arrays_b, carried, (parts_a[0],))
    x_all, g_all, hidden, grad_pre_gate, grad_pre_up = carried
    done, even_a, odd_a = first_step(parts_a[0], along_c(parts_a[1], -1), (hidden,))
    other_b, *lefts = partials_of_core(
        1, len(PAIRS), order, 1, carried[3:], weights, ranges, True, done
    )
    (done,) = return_sums((pos_a, even_a, odd_a), None, (other_b,))
    even_a, odd_a = second_hops(done)
    other_b = along_c(ordered(other_b, done), -1)
    (own_b,) = partials_of_core(1, len(PAIRS), order, 0, lefts, weights, ranges, False, done)
    done, even_b, odd_b = first_step(own_b, other_b, ())
    grad_down = weight_grad(hidden, g_all, done)
    second, third = return_sums((pos_b, even_b, odd_b), (pos_a, even_a, odd_a), (grad_down,))
    even_b, odd_b = second_hops(second)
    returned = third_hops(PAIRS[0], third)
    grad_gate = weight_grad(grad_pre_gate, x_all, (*second, *third))
    (third,) = return_sums(None, (pos_b, even_b, odd_b), (grad_gate,))
    grad_up = weight_grad(grad_pre_up, x_all, third)
    returned += third_hops(PAIRS[1], third)
    grad_tokens = add_up(returned)
    return (grad_tokens, grad_gate.T[None], grad_up.T[None], grad_down[None])


def solution(mesh):
    return jax.shard_map(
        local,
        mesh=mesh,
        in_specs=(
            P("ep", "etp"),
            P("ep", "etp"),
            P("ep", None),
            P("ep", None),
            P("ep", None, "etp"),
            P("ep", None, "etp"),
            P("ep", "etp", None),
        ),
        out_specs=(
            P("ep", "etp"),
            P("ep", None, "etp"),
            P("ep", None, "etp"),
            P("ep", "etp", None),
        ),
        check_vma=False,
    )
```
